256 devices in a mesh: rows: 8 (over x, core), clus: 32 (over y, z).
Axes of the slice: x: 4, y: 4, z: 8, core: 2. Of those that a mesh axis runs over, the one named last changes fastest.
Arguments:
- embed: bfloat16 [32768, 768], P(('rows', 'clus')), may hold values from -10 to 10
- weights: bfloat16 [32, 2736, 768], P('clus'), may hold values from -0.21875 to 0.21875
- shortlist: int32 [32768, 4], P(('rows', 'clus')), may hold values from 0 to 31, all different within a row; in each aligned block of 128 rows (0 to 127, 128 to 255, ...) at most 32 rows name the same one
- positives: int32 [32768, 8], P(('rows', 'clus')), may hold values from 0 to 10943
Outputs:
- row_grad: bfloat16 [32768, 768], P(('rows', 'clus'))
- row_loss: float32 [32768], P(('rows', 'clus'))
- weight_grad: bfloat16 [32, 2736, 768], P('clus', 'rows')
The draws below stay inside these ranges and needn't reach their ends.
Inputs may be any that keep to these rules, and one draw needn't show every extreme that they name: `shortlist`: each row names 4 different clusters. Among the rows of one device no cluster is named by more than 32 rows, a bound that some block reaches. `positives`: entry j * 2736 + l names label l of the row's j-th shortlisted cluster; a row may repeat an entry.
All inputs are finite; a program needn't handle non-finite values.
Results may differ from the reference program's by a relative error of at most 0.0034.
Values may be sent and summed in bfloat16 or wider, within the bound.
No kernel may reach another device: no remote copies, remote signals or barrier semaphores. Data moves between devices by JAX's collectives and lax.ppermute only.
A program may use at most 128 MiB of HBM per device.

```python
import math
import jax
import jax.numpy as jnp
import numpy as np
from jax import lax

D = 768
CL = 2736
K = 4
P_SIZE = 8
ROW_DEV = 128
CLUSTERS = 32
ROWS = 32768
CAP = 32


def plant(array, rng, smallest, top_value):
    extent = array.shape
    place = [jax.random.randint(jax.random.fold_in(rng, axis), (), 0, extent[axis]) for axis in range(len(extent))]
    array = array.at[tuple(place)].set(smallest)
    longest = extent.index(max(extent))
    place[longest] = (place[longest] + 1) % extent[longest]
    return array.at[tuple(place)].set(top_value)


def shard_levels(key, shape, shards, least, top_value):
    def one(dim, shards_of):
        heights = jax.random.uniform(jax.random.fold_in(jax.random.fold_in(key, 6), dim), (shards_of,), jnp.float32, least / len(shards), top_value / len(shards))
        return jnp.repeat(jnp.exp(heights), shape[dim] // shards_of).reshape((-1,) + (1,) * (len(shape) - dim - 1))

    loudness = one(*shards[0])
    for cut in shards[1:]:
        loudness = loudness * one(*cut)
    return loudness


def deal_out(stream_key, own, number, rows, amount, top, reach, skew):
    order = jax.random.permutation(stream_key, amount)
    packed, common = shares(amount, rows * top, reach, skew, True), shares(amount, rows * top, reach, skew, False)
    places = jnp.arange(amount)

    def named(lengths, turn):
        used = int((lengths > 0).sum())
        fixed = max(1, used // 4)
        passed = fixed + (places - fixed + turn * (used - fixed)) % max(1, amount - fixed)
        return jnp.zeros((amount,), jnp.int32).at[order[jnp.where(places < fixed, places, passed)]].set(jnp.asarray(lengths, jnp.int32))

    lengths = jnp.where(number % 4 == 0, named(packed, number // 4), named(common, number - number // 4 - 1))
    mixed = jax.random.permutation(jax.random.fold_in(own, 3), amount)
    donor, sink = mixed[0:amount // 2 * 2:2], mixed[1:amount // 2 * 2:2]
    slack = jnp.minimum(lengths[donor] - 1, reach - lengths[sink]) // 2
    slack = jnp.where((donor == order[0]) | (sink == order[0]) | (lengths[sink] == 0), 0, jnp.maximum(slack, 0))
    passed = jax.random.randint(jax.random.fold_in(own, 4), (amount // 2,), 0, 1 << 20) % (slack + 1)
    lengths = lengths.at[donor].add(-passed).at[sink].add(passed)
    labels = jnp.searchsorted(jnp.cumsum(lengths), jnp.arange(rows * top), side="right").astype(jnp.int32)
    listing = labels.reshape(top, rows).T
    listing = listing[jax.random.permutation(jax.random.fold_in(own, 1), rows)]
    turn = jax.random.randint(jax.random.fold_in(own, 2), (rows, 1), 0, top)
    return jnp.take_along_axis(listing, (jnp.arange(top)[None, :] + turn) % top, axis=1)


def shares(number_of, total, most, lean, full):
    loads = [(1 << 20) // math.isqrt(rank ** lean) + 1 for rank in range(1, number_of + 1)]
    largest = most if full else min(most, max(-(-total // number_of), total * loads[0] // sum(loads)))
    least = 1 if total - largest >= number_of - 1 else 0
    holding, surplus = [largest] + [least] * (number_of - 1), total - largest - least * (number_of - 1)
    while surplus > 0:
        movable = [i for i in range(1, number_of) if holding[i] < largest] or [i for i in range(1, number_of) if holding[i] < most]
        pool, left = sum([loads[i] for i in movable]), surplus
        for i in movable:
            extra = min(most - holding[i], max(1, left * loads[i] // pool), surplus)
            holding[i] = holding[i] + extra
            surplus = surplus - extra
    return np.array(holding)


def noise(rng, shape, scale, most, cuts=(), kind=jnp.bfloat16):
    level = shard_levels(rng, shape, cuts, -0.22, 0.18) if cuts else 1.0
    result = jax.random.normal(rng, shape, jnp.float32) * scale * level
    return jnp.minimum(jnp.maximum(result, -most), most).astype(kind)


def setup_inputs(seed: int = 0) -> dict:
    keys = jax.random.split(jax.random.key(seed), 5)
    embed = noise(keys[0], (ROWS, D), 2.0, 10.0, ((0, 256),))
    weights = noise(keys[1], (CLUSTERS, CL, D), D ** -0.5, 0.21875, ((0, 32),))
    shortlist_keys = jax.random.split(jax.random.fold_in(keys[2], 1), ROWS // ROW_DEV)
    shortlist_turns = jax.random.permutation(jax.random.fold_in(keys[2], 3), ROWS // ROW_DEV)
    shortlist = jax.vmap(lambda own, number: deal_out(jax.random.fold_in(keys[2], 2), own, number, ROW_DEV, CLUSTERS, K, CAP, 2))(shortlist_keys, shortlist_turns).reshape((ROWS, K))
    positives = plant(jax.random.randint(keys[3], (ROWS, P_SIZE), 0, K * CL), jax.random.fold_in(keys[3], 1), 0, (K * CL) - 1).astype(jnp.int32)
    return dict(embed=embed, weights=weights, shortlist=shortlist, positives=positives)


def targets_of(positive_ids, first_label, label_iota):
    hits = jnp.zeros((positive_ids.shape[0], label_iota.shape[0]), dtype=bool)
    for column in range(positive_ids.shape[1]):
        hits = jnp.logical_or(hits, positive_ids[:, column:column + 1] == first_label[:, None] + label_iota[None, :])
    return hits.astype(jnp.float32)


def reference(embed, weights, shortlist, positives):
    block_rows = 512
    flat_ids = shortlist.reshape(-1).astype(jnp.int32)
    order = jnp.argsort(flat_ids, stable=True).astype(jnp.int32)
    cluster_iota = jnp.arange(CLUSTERS, dtype=jnp.int32)
    counts = jnp.sum((flat_ids[:, None] == cluster_iota[None, :]).astype(jnp.int32), axis=0)
    starts = (jnp.cumsum(counts) - counts).astype(jnp.int32)
    order_pad = jnp.concatenate([order, jnp.zeros((block_rows,), jnp.int32)])
    label_iota = jnp.arange(CL, dtype=jnp.int32)
    local_iota = jnp.arange(block_rows, dtype=jnp.int32)

    def one_cluster(carry, cluster):
        grad_rows, loss_rows = carry
        table = lax.dynamic_index_in_dim(weights, cluster, 0, keepdims=False)
        count = counts[cluster]
        begin = starts[cluster]

        def going(state):
            return state[0] * block_rows < count

        def advance(state):
            blocks, grad_rows, loss_rows, total = state
            picked = lax.dynamic_slice_in_dim(order_pad, (begin + blocks * block_rows).astype(jnp.int32), block_rows)
            valid = (blocks * block_rows + local_iota) < count
            row_index = (picked // K).astype(jnp.int32)
            slot_index = (picked % K).astype(jnp.int32)
            inputs = jnp.where(valid[:, None], embed[row_index], jnp.zeros((), embed.dtype))
            scores = jnp.dot(inputs, table.T, preferred_element_type=jnp.float32)
            target = targets_of(positives[row_index], slot_index * CL, label_iota)
            losses = jnp.sum(jax.nn.softplus(scores) - target * scores, axis=1)
            loss_rows = loss_rows.at[row_index].add(jnp.where(valid, losses, jnp.zeros((), jnp.float32)))
            error = jnp.where(valid[:, None], jax.nn.sigmoid(scores) - target, jnp.zeros((), jnp.float32)).astype(jnp.bfloat16)
            grad_rows = grad_rows.at[row_index].add(jnp.dot(error, table, preferred_element_type=jnp.float32))
            total = total + lax.dot_general(error, inputs, (((0,), (0,)), ((), ())), preferred_element_type=jnp.float32)
            return blocks + 1, grad_rows, loss_rows, total

        start_state = (jnp.zeros((), jnp.int32), grad_rows, loss_rows, jnp.zeros((CL, D), jnp.float32))
        ended = lax.while_loop(going, advance, start_state)
        return (ended[1], ended[2]), ended[3].astype(jnp.bfloat16)

    start_carry = (jnp.zeros((ROWS, D), jnp.float32), jnp.zeros((ROWS,), jnp.float32))
    (grad_rows, loss_rows), weight_grad = lax.scan(one_cluster, start_carry, cluster_iota)
    return grad_rows.astype(jnp.bfloat16), loss_rows / (K * CL), weight_grad
```

```python
import functools
import jax
import jax.numpy as jnp
from jax import lax
from jax.experimental import pallas as pl
from jax.experimental.pallas import tpu as pltpu
from jax.sharding import PartitionSpec as P

BF = jnp.bfloat16
F32 = jnp.float32
LANES = 128
CHUNK = 256
HALF = 16
VMEM_LIMIT = 56 * 1024 * 1024

NT = (((1,), (1,)), ((), ()))
TN = (((0,), (0,)), ((), ()))
NN = (((1,), (0,)), ((), ()))


def dot(a, b, dims=NN):
    return lax.dot_general(a, b, dims, preferred_element_type=F32)


def iota(shape, dim):
    return lax.broadcasted_iota(jnp.int32, shape, dim)


def padded(block):
    return -(-block // 32) * 32


def pack_kernel(labels, shards, embed_ref, short_ref, pos_ref, send_ref, pick_ref):
    rows, width = embed_ref.shape
    slots_k = short_ref.shape[0]
    clusters = send_ref.shape[0]
    cap = 2 * HALF
    block = labels // shards
    extra = padded(block) - block
    short = short_ref[...]
    pos = pos_ref[...]
    count = pos.shape[0]
    cluster_id = iota((clusters, rows), 0)
    member = jnp.zeros((clusters, rows), F32)
    for j in range(slots_k):
        member += (short[j : j + 1, :] == cluster_id).astype(F32)
    before = (iota((rows, rows), 0) < iota((rows, rows), 1)).astype(BF)
    rank = dot(member.astype(BF), before)
    code = jnp.where(member > 0.5, rank, -1.0)
    slot = iota((clusters, cap, rows), 1).astype(F32)
    pick = (code[:, None, :] == slot).astype(F32)
    pick = pick.reshape(clusters * cap, rows).astype(BF)
    pick_ref[...] = pick
    values, names = [], []
    for j in range(slots_k):
        local = pos - j * labels
        inside = jnp.logical_and(local >= 0, local < labels)
        shard = jnp.zeros_like(local)
        for b in range(1, shards):
            shard += (local >= b * block).astype(jnp.int32)
        column = jnp.where(inside, local + extra * shard, 0)
        bit = lax.shift_left(jnp.ones_like(column), lax.shift_right_logical(column, 7))
        values.append(jnp.where(inside, bit, 0).astype(F32))
        values.append(jnp.bitwise_and(column, LANES - 1).astype(F32))
        names.append(jnp.broadcast_to(short[j : j + 1, :], (2 * count, rows)).astype(F32))
    used = 2 * count * slots_k
    rest = jnp.zeros((LANES - used, rows), F32)
    values = jnp.concatenate(values + [rest], axis=0).astype(BF)
    names = jnp.concatenate(names + [rest], axis=0).astype(BF)
    got_values = dot(pick, values, NT)
    got_names = dot(pick, names, NT)
    own = lax.shift_right_logical(iota(got_values.shape, 0), 5).astype(F32)
    kept = jnp.where(got_names == own, got_values, 0.0).astype(BF)
    kept = kept.reshape(clusters, cap, LANES)
    source = iota((LANES, LANES), 0)
    target = iota((LANES, LANES), 1)
    folded = jnp.bitwise_and(source, 2 * count - 1)
    valid = source < used
    fold_a = jnp.logical_and(valid, folded == target).astype(BF)
    fold_b = jnp.logical_and(valid, folded + 2 * count == target).astype(BF)
    meta = dot(kept[:, :HALF].reshape(clusters * HALF, LANES), fold_a)
    meta += dot(kept[:, HALF:].reshape(clusters * HALF, LANES), fold_b)
    got = dot(pick, embed_ref[...]).astype(BF).reshape(clusters, cap, width)
    send_ref[:, :, :width] = got[:, :HALF]
    send_ref[:, :, width : 2 * width] = got[:, HALF:]
    send_ref[:, :, 2 * width :] = meta.astype(BF).reshape(clusters, HALF, LANES)


def log1p(p):
    small = p * (1.0 - p * (0.5 - p * (1.0 / 3.0 - p * 0.25)))
    return jnp.where(p < 0.01, small, jnp.log(1.0 + p))


def compute_kernel(
    count, core_ref, recv_ref, weight_ref, real_ref, back_ref, keep_ref, give_ref,
    rows_ref, bits_ref, s_a, s_b, e_a, e_b, grad_ref, wgrad_ref, relu_ref, prod_ref,
):
    sources = recv_ref.shape[0]
    width = rows_ref.shape[1]
    total = rows_ref.shape[0]
    chunks = weight_ref.shape[0] // CHUNK
    rows3 = jnp.concatenate(
        [recv_ref[:, :, :width], recv_ref[:, :, width : 2 * width]], axis=1
    )
    rows_ref[...] = rows3.reshape(total, width)
    step = 8
    for start in range(0, sources, step):
        meta = recv_ref[start : start + step, :, 2 * width :].astype(F32).astype(jnp.int32)
        meta = meta.reshape(step * HALF, LANES)
        lane = iota((step * HALF, LANES), 1)
        halves = []
        for base in (0, 2 * count):
            bits = jnp.zeros((step * HALF, LANES), jnp.int32)
            for p in range(count):
                value = meta[:, base + p : base + p + 1]
                place = meta[:, base + count + p : base + count + p + 1]
                bits = jnp.bitwise_or(bits, jnp.where(place == lane, value, 0))
            halves.append(bits.reshape(step, HALF, LANES))
        both = jnp.concatenate(halves, axis=1)
        bits_ref[start * 2 * HALF : (start + step) * 2 * HALF] = both.reshape(-1, LANES)
    grad_ref[...] = jnp.zeros_like(grad_ref)
    relu_ref[...] = jnp.zeros_like(relu_ref)
    prod_ref[...] = jnp.zeros_like(prod_ref)

    def weight(i):
        return weight_ref[pl.ds(pl.multiple_of(i * CHUNK, CHUNK), CHUNK), :]

    def score(i, s_ref):
        s_ref[...] = dot(rows_ref[...], weight(i), NT)

    def pointwise(i, s_ref, e_ref):
        tall = 64
        for start in range(0, total, tall):
            here = slice(start, start + tall)
            bits = bits_ref[here]
            relu = relu_ref[here]
            prod = prod_ref[here]
            for part in range(CHUNK // LANES):
                lanes = slice(part * LANES, (part + 1) * LANES)
                real = real_ref[i * (CHUNK // LANES) + part]
                s = s_ref[here, lanes]
                hit = lax.shift_left(bits, 31 - (i * (CHUNK // LANES) + part)) < 0
                v = jnp.where(hit, -s, s)
                e = jnp.exp(-jnp.abs(s))
                d = 1.0 + e
                r = pl.reciprocal(d, approx=True)
                r = r * (2.0 - d * r)
                sig = jnp.where(v >= 0.0, r, e * r)
                e_ref[here, lanes] = jnp.where(hit, -sig, sig).astype(BF)
                relu = relu + jnp.maximum(v, 0.0)
                prod = prod + (e * real) * (1.0 + prod)
            relu_ref[here] = relu
            prod_ref[here] = prod

    def gradients(i, e_ref):
        e = e_ref[...]
        grad_ref[...] += dot(e, weight(i))
        wgrad_ref[pl.ds(pl.multiple_of(i * CHUNK, CHUNK), CHUNK), :] = dot(e, rows_ref[...], TN)

    score(0, s_a)
    score(1, s_b)
    pointwise(0, s_a, e_a)

    def pair(k, carry):
        i = 2 * k + 1
        score(i + 1, s_a)
        pointwise(i, s_b, e_b)
        gradients(i - 1, e_a)
        score(i + 2, s_b)
        pointwise(i + 1, s_a, e_a)
        gradients(i, e_b)
        return carry

    lax.fori_loop(0, (chunks - 3) // 2, pair, 0)
    last = chunks - 1
    score(last, s_a)
    pointwise(last - 1, s_b, e_b)
    gradients(last - 2, e_a)
    pointwise(last, s_a, e_a)
    gradients(last - 1, e_b)
    gradients(last, e_a)

    grads = grad_ref[...].astype(BF).reshape(sources, 2 * HALF, width)
    back_ref[:, :, :width] = grads[:, :HALF]
    back_ref[:, :, width : 2 * width] = grads[:, HALF:]
    loss = jnp.sum(relu_ref[...] + log1p(prod_ref[...]), axis=1, keepdims=True)
    first = loss.astype(BF).astype(F32)
    second = (loss - first).astype(BF).astype(F32)
    third = loss - first - second
    lane = iota((total, LANES), 1)
    part = jnp.bitwise_and(lane, 3)
    terms = jnp.where(part == 0, first, jnp.where(part == 1, second, jnp.where(part == 2, third, 0.0)))
    terms = terms.reshape(sources, 2 * HALF, LANES)
    side = iota((sources, HALF, LANES), 2)
    mixed = jnp.where(
        side < 4, terms[:, :HALF], jnp.where(side < 8, terms[:, HALF:], 0.0)
    )
    back_ref[:, :, 2 * width :] = mixed.astype(BF)

    me = core_ref[0]
    shards, block, _ = keep_ref.shape
    for x in range(shards):
        mine = pl.multiple_of((2 * x + me) * block, 32)
        other = pl.multiple_of((2 * x + 1 - me) * block, 32)
        keep_ref[x] = wgrad_ref[pl.ds(mine, block), :]
        give_ref[x] = wgrad_ref[pl.ds(other, block), :].astype(BF)


def combine_kernel(scale, got_ref, pick_ref, grad_ref, loss_ref):
    clusters = got_ref.shape[0]
    width = grad_ref.shape[1]
    rows = grad_ref.shape[0]
    pick = pick_ref[...].reshape(clusters, 2 * HALF, rows)
    pick_a = pick[:, :HALF].reshape(clusters * HALF, rows)
    pick_b = pick[:, HALF:].reshape(clusters * HALF, rows)

    def lanes(start, size):
        return got_ref[:, :, start : start + size].reshape(clusters * HALF, size)

    grads = dot(pick_a, lanes(0, width), TN) + dot(pick_b, lanes(width, width), TN)
    grad_ref[...] = grads.astype(BF)
    terms = lanes(2 * width, LANES)
    first = dot(terms, pick_a, TN)
    second = dot(terms, pick_b, TN)
    loss = jnp.sum(first[:4], axis=0, keepdims=True) + jnp.sum(second[4:8], axis=0, keepdims=True)
    loss_ref[...] = loss * scale


def whole(shape, dtype):
    return jax.ShapeDtypeStruct(shape, dtype)


VM = pl.BlockSpec(memory_space=pltpu.VMEM)
SM = pl.BlockSpec(memory_space=pltpu.SMEM)
PARAMS = pltpu.CompilerParams(vmem_limit_bytes=VMEM_LIMIT)


def local(embed, weights, shortlist, positives):
    rows, width = embed.shape
    slots_k = shortlist.shape[1]
    count = positives.shape[1]
    _, labels, _ = weights.shape
    clusters = lax.axis_size("clus")
    shards = lax.axis_size("rows")
    wide = 2 * width + LANES
    total = clusters * 2 * HALF
    block = labels // shards
    tall = padded(block)
    half = shards // 2

    send, pick = pl.pallas_call(
        functools.partial(pack_kernel, labels, shards),
        out_shape=(whole((clusters, HALF, wide), BF), whole((total, rows), BF)),
        in_specs=[VM] * 3,
        out_specs=(VM, VM),
        compiler_params=PARAMS,
    )(embed, shortlist.T, positives.T)
    recv = lax.all_to_all(send, "clus", 0, 0, tiled=True)

    table = jnp.pad(weights.reshape(shards, block, width), ((0, 0), (0, tall - block), (0, 0)))
    table = table.reshape(shards * tall, width)
    column = jnp.arange(shards * tall, dtype=jnp.int32)
    real = (column % tall < block).astype(F32).reshape(-1, 1, LANES)
    place = lax.axis_index("rows")
    core = place % 2
    back, keep, give = pl.pallas_call(
        functools.partial(compute_kernel, count),
        out_shape=(
            whole((clusters, HALF, wide), BF),
            whole((half, tall, width), F32),
            whole((half, tall, width), BF),
        ),
        in_specs=[SM, VM, VM, VM],
        out_specs=(VM, VM, VM),
        scratch_shapes=[
            pltpu.VMEM((total, width), BF),
            pltpu.VMEM((total, LANES), jnp.int32),
            pltpu.VMEM((total, CHUNK), F32),
            pltpu.VMEM((total, CHUNK), F32),
            pltpu.VMEM((total, CHUNK), BF),
            pltpu.VMEM((total, CHUNK), BF),
            pltpu.VMEM((total, width), F32),
            pltpu.VMEM((shards * tall, width), F32),
            pltpu.VMEM((total, LANES), F32),
            pltpu.VMEM((total, LANES), F32),
        ],
        compiler_params=PARAMS,
    )(core.reshape(1), recv, table, real)

    taken = lax.ppermute(give, "rows", [(i, i ^ 1) for i in range(shards)])
    pair = keep + taken.astype(F32)
    x = place // 2

    def piece(k):
        return lax.dynamic_index_in_dim(pair, (x + k) % half, 0, keepdims=False)

    share = piece(0)
    arrived = []
    for k in range(1, half):
        perm = [(i, (i + 2 * k) % shards) for i in range(shards)]
        arrived.append(lax.ppermute(piece(k).astype(BF), "rows", perm))

    got = lax.all_to_all(back, "clus", 0, 0, tiled=True)
    row_grad, row_loss = pl.pallas_call(
        functools.partial(combine_kernel, 1.0 / (slots_k * labels)),
        out_shape=(whole((rows, width), BF), whole((1, rows), F32)),
        in_specs=[VM] * 2,
        out_specs=(VM, VM),
        compiler_params=PARAMS,
    )(got, pick)

    for part in arrived:
        share = share + part.astype(F32)
    weight_grad = share[:block].astype(BF)[None]
    return row_grad, row_loss.reshape(rows), weight_grad


def solution(mesh):
    placed = (
        P(("rows", "clus"), None),
        P("clus", None, None),
        P(("rows", "clus"), None),
        P(("rows", "clus"), None),
    )
    return jax.shard_map(
        local,
        mesh=mesh,
        in_specs=placed,
        out_specs=(P(("rows", "clus"), None), P(("rows", "clus")), P("clus", "rows", None)),
        check_vma=False,
    )
```

```python
import functools
import jax
import jax.numpy as jnp
import numpy as np
from jax import lax
from jax.experimental import pallas as pl
from jax.experimental.pallas import tpu as pltpu
from jax.sharding import PartitionSpec as P

BF = jnp.bfloat16
F32 = jnp.float32
LANES = 128
CHUNK = 256
HALF = 16
VMEM_LIMIT = 40 * 1024 * 1024
TALL = 32
BLOCK = 512
LOG2E = 1.4426950408889634

NT = (((1,), (1,)), ((), ()))
TN = (((0,), (0,)), ((), ()))
NN = (((1,), (0,)), ((), ()))


def dot(a, b, dims=NN):
    return lax.dot_general(a, b, dims, preferred_element_type=F32)


def iota(shape, dim):
    return lax.broadcasted_iota(jnp.int32, shape, dim)


def padded(block):
    return -(-block // 32) * 32


def pack_kernel(labels, shards, shift_ref, embed_ref, short_ref, pos_ref, send_ref, pick_ref):
    rows, width = embed_ref.shape
    slots_k = short_ref.shape[0]
    clusters = send_ref.shape[0]
    cap = 2 * HALF
    block = labels // shards
    short = short_ref[...]
    pos = pos_ref[...]
    count = pos.shape[0]
    cluster_id = iota((clusters, rows), 0)
    member = jnp.zeros((clusters, rows), F32)
    for j in range(slots_k):
        member += (short[j : j + 1, :] == cluster_id).astype(F32)
    before = (iota((rows, rows), 0) < iota((rows, rows), 1)).astype(BF)
    rank = dot(member.astype(BF), before)
    code = jnp.where(member > 0.5, rank, -1.0)
    slot = iota((clusters, cap, rows), 1).astype(F32)
    pick = (code[:, None, :] == slot).astype(F32)
    pick = pick.reshape(clusters * cap, rows).astype(BF)
    pick_ref[...] = pick
    values, names = [], []
    for j in range(slots_k):
        local = pos - j * labels
        inside = jnp.logical_and(local >= 0, local < labels)
        column = local + shift_ref[0]
        for b in range(1, shards):
            column += jnp.where(local >= b * block, shift_ref[b] - shift_ref[b - 1], 0)
        column = jnp.where(inside, column, 0)
        bit = lax.shift_left(jnp.ones_like(column), lax.shift_right_logical(column, 7))
        values.append(jnp.where(inside, bit, 0).astype(F32))
        values.append(jnp.bitwise_and(column, LANES - 1).astype(F32))
        names.append(jnp.broadcast_to(short[j : j + 1, :], (2 * count, rows)).astype(F32))
    used = 2 * count * slots_k
    rest = jnp.zeros((LANES - used, rows), F32)
    values = jnp.concatenate(values + [rest], axis=0).astype(BF)
    names = jnp.concatenate(names + [rest], axis=0).astype(BF)
    got_values = dot(pick, values, NT)
    got_names = dot(pick, names, NT)
    own = lax.shift_right_logical(iota(got_values.shape, 0), 5).astype(F32)
    kept = jnp.where(got_names == own, got_values, 0.0).astype(BF)
    kept = kept.reshape(clusters, cap, LANES)
    source = iota((LANES, LANES), 0)
    target = iota((LANES, LANES), 1)
    folded = jnp.bitwise_and(source, 2 * count - 1)
    valid = source < used
    fold_a = jnp.logical_and(valid, folded == target).astype(BF)
    fold_b = jnp.logical_and(valid, folded + 2 * count == target).astype(BF)
    meta = dot(kept[:, :HALF].reshape(clusters * HALF, LANES), fold_a)
    meta += dot(kept[:, HALF:].reshape(clusters * HALF, LANES), fold_b)
    got = dot(pick, embed_ref[...]).astype(BF).reshape(clusters, cap, width)
    send_ref[:, :, :width] = got[:, :HALF]
    send_ref[:, :, width : 2 * width] = got[:, HALF:]
    send_ref[:, :, 2 * width :] = meta.astype(BF).reshape(clusters, HALF, LANES)


def assemble(recv_ref, rows_ref):
    total, width = rows_ref.shape
    left, right = recv_ref[:, :, :width], recv_ref[:, :, width : 2 * width]
    rows_ref[...] = jnp.concatenate([left, right], axis=1).reshape(total, width)


def target_bits(count, recv_ref, bits_ref, width):
    sources = recv_ref.shape[0]
    step = 8
    for start in range(0, sources, step):
        meta = recv_ref[start : start + step, :, 2 * width :].astype(F32).astype(jnp.int32)
        meta = meta.reshape(step * HALF, LANES)
        lane = iota((step * HALF, LANES), 1)
        halves = []
        for base in (0, 2 * count):
            bits = jnp.zeros((step * HALF, LANES), jnp.int32)
            for p in range(count):
                value = meta[:, base + p : base + p + 1]
                place = meta[:, base + count + p : base + count + p + 1]
                bits = jnp.bitwise_or(bits, jnp.where(place == lane, value, 0))
            halves.append(bits.reshape(step, HALF, LANES))
        both = jnp.concatenate(halves, axis=1)
        bits_ref[start * 2 * HALF : (start + step) * 2 * HALF] = both.reshape(-1, LANES)


def score_kernel(
    count, recv_ref, weight_ref, pads_ref, back_ref, error_out,
    rows_ref, bits_ref, s_ref, error_ref, relu_ref, prod_ref, sum_ref, sem,
):
    sources = recv_ref.shape[0]
    total, width = rows_ref.shape
    chunks = weight_ref.shape[0] // CHUNK
    assemble(recv_ref, rows_ref)
    target_bits(count, recv_ref, bits_ref, width)
    copies = []

    def score(i, at):
        chunk = weight_ref[i * CHUNK : (i + 1) * CHUNK]
        s_ref[i % 2, at] = dot(rows_ref[at], chunk, NT)

    def pointwise(i, at):
        for start in range(at.start, at.stop, TALL):
            here = slice(start, start + TALL)
            bits = bits_ref[here]
            if i == 0:
                relu = jnp.zeros((TALL, LANES), F32)
                prod = jnp.ones((TALL, LANES), F32)
                summed = relu
            else:
                relu, prod, summed = relu_ref[here], prod_ref[here], sum_ref[here]
            for part in range(CHUNK // LANES):
                column = i * CHUNK + part * LANES
                s = s_ref[i % 2, here, part * LANES : (part + 1) * LANES]
                hit = lax.shift_left(bits, 31 - column // LANES) < 0
                size = jnp.abs(s)
                e = jnp.exp2(size * -LOG2E)
                d = 1.0 + e
                r = pl.reciprocal(d, approx=True)
                up = jnp.logical_xor(s >= 0.0, hit)
                chance = jnp.where(up, r, e * r)
                error = jnp.where(hit, -chance, chance)
                error_ref[here, column : column + LANES] = error.astype(BF)
                relu = relu + jnp.where(up, size, 0.0)
                prod = prod * d
                summed = summed + e
            relu_ref[here] = relu
            prod_ref[here] = prod
            sum_ref[here] = summed

    blocks = [slice(k, k + BLOCK) for k in range(0, total, BLOCK)]
    for i in range(-1, chunks):
        for at in blocks:
            if i + 1 < chunks:
                score(i + 1, at)
            if i >= 0:
                pointwise(i, at)
        if i >= 0:
            columns = slice(i * CHUNK, (i + 1) * CHUNK)
            copy = pltpu.make_async_copy(
                error_ref.at[:, columns], error_out.at[:, columns], sem.at[i]
            )
            copy.start()
            copies.append(copy)
    for at in blocks:
        first, last = at.start // (2 * HALF), at.stop // (2 * HALF)
        grads = dot(error_ref[at], weight_ref[...]).astype(BF)
        grads = grads.reshape(last - first, 2 * HALF, width)
        back_ref[first:last, :, :width] = grads[:, :HALF]
        back_ref[first:last, :, width : 2 * width] = grads[:, HALF:]

    summed = sum_ref[...] - pads_ref[0:1]
    tail = jnp.where(summed < 4e-4, summed, jnp.log(prod_ref[...] * pads_ref[1:2]))
    loss = jnp.sum(relu_ref[...] + tail, axis=1, keepdims=True)
    first = loss.astype(BF).astype(F32)
    second = (loss - first).astype(BF).astype(F32)
    third = loss - first - second
    part = jnp.bitwise_and(iota((total, LANES), 1), 3)
    terms = jnp.where(part == 2, third, 0.0)
    terms = jnp.where(part == 1, second, terms)
    terms = jnp.where(part == 0, first, terms)
    terms = terms.reshape(sources, 2 * HALF, LANES)
    side = iota((sources, HALF, LANES), 2)
    mixed = jnp.where(side < 8, terms[:, HALF:], 0.0)
    mixed = jnp.where(side < 4, terms[:, :HALF], mixed)
    back_ref[:, :, 2 * width :] = mixed.astype(BF)
    for copy in copies:
        copy.wait()


def weight_kernel(error_ref, recv_ref, out_ref, rows_ref):
    assemble(recv_ref, rows_ref)
    labels = out_ref.shape[0]
    for start in range(0, labels, 2 * CHUNK):
        here = slice(start, min(start + 2 * CHUNK, labels))
        out_ref[here] = dot(error_ref[:, here], rows_ref[...], TN).astype(out_ref.dtype)


def combine_kernel(scale, got_ref, pick_ref, grad_ref, loss_ref):
    clusters = got_ref.shape[0]
    width = grad_ref.shape[1]
    rows = grad_ref.shape[0]
    pick = pick_ref[...].reshape(clusters, 2 * HALF, rows)
    pick_a = pick[:, :HALF].reshape(clusters * HALF, rows)
    pick_b = pick[:, HALF:].reshape(clusters * HALF, rows)

    def lanes(start, size):
        return got_ref[:, :, start : start + size].reshape(clusters * HALF, size)

    grads = dot(pick_a, lanes(0, width), TN) + dot(pick_b, lanes(width, width), TN)
    grad_ref[...] = grads.astype(BF)
    terms = lanes(2 * width, LANES)
    first = dot(terms, pick_a, TN)
    second = dot(terms, pick_b, TN)
    loss = jnp.sum(first[:4], axis=0, keepdims=True) + jnp.sum(second[4:8], axis=0, keepdims=True)
    loss_ref[...] = loss * scale


def whole(shape, dtype):
    return jax.ShapeDtypeStruct(shape, dtype)


VM = pl.BlockSpec(memory_space=pltpu.VMEM)
SM = pl.BlockSpec(memory_space=pltpu.SMEM)
PARAMS = pltpu.CompilerParams(vmem_limit_bytes=VMEM_LIMIT)


def local(embed, weights, shortlist, positives):
    rows, width = embed.shape
    slots_k = shortlist.shape[1]
    count = positives.shape[1]
    _, labels, _ = weights.shape
    clusters = lax.axis_size("clus")
    shards = lax.axis_size("rows")
    wide = 2 * width + LANES
    total = clusters * 2 * HALF
    block = labels // shards
    tall = padded(block)
    half = shards // 2

    place = lax.axis_index("rows")
    core, x = place % 2, place // 2
    order = [((x + k) % half) * 2 + side for side in (1 - core, core) for k in range(half)]
    shard = jnp.arange(shards, dtype=jnp.int32)
    step = (shard // 2 - x + half) % half
    slot = jnp.where(shard % 2 == core, half + step, step)
    shift = (tall * slot - block * shard).astype(jnp.int32)

    send, pick = pl.pallas_call(
        functools.partial(pack_kernel, labels, shards),
        out_shape=(whole((clusters, HALF, wide), BF), whole((total, rows), BF)),
        in_specs=[SM] + [VM] * 3,
        out_specs=(VM, VM),
        compiler_params=PARAMS,
    )(shift, embed, shortlist.T, positives.T)
    recv = lax.all_to_all(send, "clus", 0, 0, tiled=True)

    table = jnp.pad(weights.reshape(shards, block, width), ((0, 0), (0, tall - block), (0, 0)))
    table = jnp.stack([lax.dynamic_index_in_dim(table, k, 0, keepdims=False) for k in order])
    table = table.reshape(shards * tall, width)
    column = np.arange(shards * tall)
    pads = np.bincount(column[column % tall >= block] % LANES, minlength=LANES)
    pads = np.stack([pads, 0.5**pads]).astype(np.float32)
    back, error = pl.pallas_call(
        functools.partial(score_kernel, count),
        out_shape=(whole((clusters, HALF, wide), BF), whole((total, shards * tall), BF)),
        in_specs=[VM, VM, VM],
        out_specs=(VM, pl.BlockSpec(memory_space=pl.ANY)),
        scratch_shapes=[
            pltpu.VMEM((total, width), BF),
            pltpu.VMEM((total, LANES), jnp.int32),
            pltpu.VMEM((2, total, CHUNK), F32),
            pltpu.VMEM((total, shards * tall), BF),
            pltpu.VMEM((total, LANES), F32),
            pltpu.VMEM((total, LANES), F32),
            pltpu.VMEM((total, LANES), F32),
            pltpu.SemaphoreType.DMA((shards * tall // CHUNK,)),
        ],
        compiler_params=PARAMS,
    )(recv, table, jnp.asarray(pads))
    got = lax.all_to_all(back, "clus", 0, 0, tiled=True)

    def weight_part(index, dtype):
        size = half * tall
        work = total * size * width
        return pl.pallas_call(
            weight_kernel,
            grid=(1,),
            out_shape=whole((size, width), dtype),
            in_specs=[
                pl.BlockSpec((total, size), lambda i: (0, index)),
                pl.BlockSpec((clusters, HALF, wide), lambda i: (0, 0, 0)),
            ],
            out_specs=pl.BlockSpec((size, width), lambda i: (0, 0)),
            scratch_shapes=[pltpu.VMEM((total, width), BF)],
            compiler_params=PARAMS,
            cost_estimate=pl.CostEstimate(
                flops=2 * work, bytes_accessed=8 * 1024 * 1024, transcendentals=0
            ),
        )(error, recv)

    give = weight_part(0, BF)
    taken = lax.ppermute(give, "rows", [(i, i ^ 1) for i in range(shards)])
    keep = weight_part(1, F32)

    def piece(k):
        here = slice(k * tall, (k + 1) * tall)
        return keep[here] + taken[here].astype(F32)

    arrived = []
    for k in (2, 1, 3):
        perm = [(i, (i + 2 * k) % shards) for i in range(shards)]
        arrived.append(lax.ppermute(piece(k).astype(BF), "rows", perm))
    share = piece(0)

    row_grad, row_loss = pl.pallas_call(
        functools.partial(combine_kernel, 1.0 / (slots_k * labels)),
        out_shape=(whole((rows, width), BF), whole((1, rows), F32)),
        in_specs=[VM] * 2,
        out_specs=(VM, VM),
        compiler_params=PARAMS,
    )(got, pick)

    for part in arrived:
        share = share + part.astype(F32)
    weight_grad = share[:block].astype(BF)[None]
    return row_grad, row_loss.reshape(rows), weight_grad


def solution(mesh):
    placed = (
        P(("rows", "clus"), None),
        P("clus", None, None),
        P(("rows", "clus"), None),
        P(("rows", "clus"), None),
    )
    return jax.shard_map(
        local,
        mesh=mesh,
        in_specs=placed,
        out_specs=(P(("rows", "clus"), None), P(("rows", "clus")), P("clus", "rows", None)),
        check_vma=False,
    )
```

```python
import functools
import jax
import jax.numpy as jnp
import numpy as np
from jax import lax
from jax.experimental import pallas as pl
from jax.experimental.pallas import tpu as pltpu
from jax.sharding import PartitionSpec as P

BF = jnp.bfloat16
F32 = jnp.float32
LANES = 128
CHUNK = 256
HALF = 16
VMEM_LIMIT = 40 * 1024 * 1024
TALL = 32
BLOCK = 512
LOG2E = 1.4426950408889634

NT = (((1,), (1,)), ((), ()))
TN = (((0,), (0,)), ((), ()))
NN = (((1,), (0,)), ((), ()))


def dot(a, b, dims=NN):
    return lax.dot_general(a, b, dims, preferred_element_type=F32)


def iota(shape, dim):
    return lax.broadcasted_iota(jnp.int32, shape, dim)


def padded(block):
    return -(-block // 32) * 32


def pack_kernel(labels, shards, embed_ref, short_ref, pos_ref, send_ref, pick_ref):
    rows, width = embed_ref.shape
    slots_k = short_ref.shape[0]
    clusters = send_ref.shape[0]
    cap = 2 * HALF
    block = labels // shards
    place = lax.axis_index("rows")
    core, x = lax.rem(place, 2), lax.div(place, 2)
    half = shards // 2
    shift = []
    for b in range(shards):
        step = lax.rem(b // 2 - x + half, half)
        slot = step + jnp.where(core == b % 2, half, 0)
        shift.append(padded(block) * slot - block * b)
    short = short_ref[...]
    pos = pos_ref[...]
    count = pos.shape[0]
    cluster_id = iota((clusters, rows), 0)
    member = jnp.zeros((clusters, rows), F32)
    for j in range(slots_k):
        member += (short[j : j + 1, :] == cluster_id).astype(F32)
    before = (iota((rows, rows), 0) < iota((rows, rows), 1)).astype(BF)
    rank = dot(member.astype(BF), before)
    code = jnp.where(member > 0.5, rank, -1.0)
    slot = iota((clusters, cap, rows), 1).astype(F32)
    pick = (code[:, None, :] == slot).astype(F32)
    pick = pick.reshape(clusters * cap, rows).astype(BF)
    pick_ref[...] = pick
    values, names = [], []
    for j in range(slots_k):
        local = pos - j * labels
        inside = jnp.logical_and(local >= 0, local < labels)
        column = local + shift[0]
        for b in range(1, shards):
            column += jnp.where(local >= b * block, shift[b] - shift[b - 1], 0)
        column = jnp.where(inside, column, 0)
        bit = lax.shift_left(jnp.ones_like(column), lax.shift_right_logical(column, 7))
        values.append(jnp.where(inside, bit, 0).astype(F32))
        values.append(jnp.bitwise_and(column, LANES - 1).astype(F32))
        names.append(jnp.broadcast_to(short[j : j + 1, :], (2 * count, rows)).astype(F32))
    used = 2 * count * slots_k
    rest = jnp.zeros((LANES - used, rows), F32)
    values = jnp.concatenate(values + [rest], axis=0).astype(BF)
    names = jnp.concatenate(names + [rest], axis=0).astype(BF)
    got_values = dot(pick, values, NT)
    got_names = dot(pick, names, NT)
    own = lax.shift_right_logical(iota(got_values.shape, 0), 5).astype(F32)
    kept = jnp.where(got_names == own, got_values, 0.0).astype(BF)
    kept = kept.reshape(clusters, cap, LANES)
    source = iota((LANES, LANES), 0)
    target = iota((LANES, LANES), 1)
    folded = jnp.bitwise_and(source, 2 * count - 1)
    valid = source < used
    fold_a = jnp.logical_and(valid, folded == target).astype(BF)
    fold_b = jnp.logical_and(valid, folded + 2 * count == target).astype(BF)
    meta = dot(kept[:, :HALF].reshape(clusters * HALF, LANES), fold_a)
    meta += dot(kept[:, HALF:].reshape(clusters * HALF, LANES), fold_b)
    got = dot(pick, embed_ref[...]).astype(BF).reshape(clusters, cap, width)
    send_ref[:, :, :width] = got[:, :HALF]
    send_ref[:, :, width : 2 * width] = got[:, HALF:]
    send_ref[:, :, 2 * width :] = meta.astype(BF).reshape(clusters, HALF, LANES)


def assemble(recv_ref, rows_ref):
    total, width = rows_ref.shape
    left, right = recv_ref[:, :, :width], recv_ref[:, :, width : 2 * width]
    rows_ref[...] = jnp.concatenate([left, right], axis=1).reshape(total, width)


def target_bits(count, recv_ref, bits_ref, width):
    sources = recv_ref.shape[0]
    step = 8
    for start in range(0, sources, step):
        meta = recv_ref[start : start + step, :, 2 * width :].astype(F32).astype(jnp.int32)
        meta = meta.reshape(step * HALF, LANES)
        lane = iota((step * HALF, LANES), 1)
        halves = []
        for base in (0, 2 * count):
            bits = jnp.zeros((step * HALF, LANES), jnp.int32)
            for p in range(count):
                value = meta[:, base + p : base + p + 1]
                place = meta[:, base + count + p : base + count + p + 1]
                bits = jnp.bitwise_or(bits, jnp.where(place == lane, value, 0))
            halves.append(bits.reshape(step, HALF, LANES))
        both = jnp.concatenate(halves, axis=1)
        bits_ref[start * 2 * HALF : (start + step) * 2 * HALF] = both.reshape(-1, LANES)


def score_kernel(
    count, recv_ref, table_ref, pads_ref, back_out, give_out, keep_out,
    weight_ref, back_ref, rows_ref, bits_ref, s_ref, error_ref, relu_ref, prod_ref, sum_ref,
    weight_sem, error_sem, back_sem, rows_sem,
):
    sources = recv_ref.shape[0]
    total, width = rows_ref.shape
    chunks = weight_ref.shape[0] // CHUNK
    loads = []
    for i in range(chunks):
        here = slice(i * CHUNK, (i + 1) * CHUNK)
        load = pltpu.make_async_copy(table_ref.at[here], weight_ref.at[here], weight_sem.at[i])
        load.start()
        loads.append(load)
    assemble(recv_ref, rows_ref)
    spare = pltpu.make_async_copy(rows_ref, give_out.at[:, keep_out.shape[1] :], rows_sem)
    spare.start()
    target_bits(count, recv_ref, bits_ref, width)
    copies = [spare]

    def score(i, at):
        chunk = weight_ref[i * CHUNK : (i + 1) * CHUNK]
        s_ref[i % 2, at] = dot(rows_ref[at], chunk, NT)

    def pointwise(i, at):
        for start in range(at.start, at.stop, TALL):
            here = slice(start, start + TALL)
            bits = bits_ref[here]
            if i == 0:
                relu = jnp.zeros((TALL, LANES), F32)
                prod = jnp.ones((TALL, LANES), F32)
                summed = relu
            else:
                relu, prod, summed = relu_ref[here], prod_ref[here], sum_ref[here]
            for part in range(CHUNK // LANES):
                column = i * CHUNK + part * LANES
                s = s_ref[i % 2, here, part * LANES : (part + 1) * LANES]
                hit = lax.shift_left(bits, 31 - column // LANES) < 0
                size = jnp.abs(s)
                e = jnp.exp2(size * -LOG2E)
                d = 1.0 + e
                r = pl.reciprocal(d, approx=True)
                up = jnp.logical_xor(s >= 0.0, hit)
                chance = jnp.where(up, r, e * r)
                error = jnp.where(hit, -chance, chance)
                error_ref[here, column : column + LANES] = error.astype(BF)
                relu = relu + jnp.where(up, size, 0.0)
                prod = prod * d
                summed = summed + e
            relu_ref[here] = relu
            prod_ref[here] = prod
            sum_ref[here] = summed

    def flush(at):
        half = keep_out.shape[1]
        for k, out in enumerate((give_out, keep_out)):
            copy = pltpu.make_async_copy(
                error_ref.at[at, k * half : (k + 1) * half],
                out.at[at, :half],
                error_sem.at[2 * (at.start // BLOCK) + k],
            )
            copy.start()
            copies.append(copy)

    blocks = [slice(k, k + BLOCK) for k in range(0, total, BLOCK)]
    for i in range(-1, chunks):
        if i + 1 < chunks:
            loads[i + 1].wait()
        for at in blocks:
            if i + 1 < chunks:
                score(i + 1, at)
            if i >= 0:
                pointwise(i, at)
    for at in blocks:
        flush(at)

    summed = sum_ref[...] - pads_ref[0:1]
    tail = jnp.where(summed < 4e-4, summed, jnp.log(prod_ref[...] * pads_ref[1:2]))
    loss = jnp.sum(relu_ref[...] + tail, axis=1, keepdims=True)
    first = loss.astype(BF).astype(F32)
    second = (loss - first).astype(BF).astype(F32)
    third = loss - first - second
    part = jnp.bitwise_and(iota((total, LANES), 1), 3)
    terms = jnp.where(part == 2, third, 0.0)
    terms = jnp.where(part == 1, second, terms)
    terms = jnp.where(part == 0, first, terms)
    terms = terms.reshape(sources, 2 * HALF, LANES)
    side = iota((sources, HALF, LANES), 2)
    mixed = jnp.where(side < 8, terms[:, HALF:], 0.0)
    mixed = jnp.where(side < 4, terms[:, :HALF], mixed)
    back_ref[:, :, 2 * width :] = mixed.astype(BF)
    for at in blocks:
        first, last = at.start // (2 * HALF), at.stop // (2 * HALF)
        grads = dot(error_ref[at], weight_ref[...]).astype(BF)
        grads = grads.reshape(last - first, 2 * HALF, width)
        back_ref[first:last, :, :width] = grads[:, :HALF]
        back_ref[first:last, :, width : 2 * width] = grads[:, HALF:]
        copy = pltpu.make_async_copy(
            back_ref.at[first:last], back_out.at[first:last], back_sem.at[at.start // BLOCK]
        )
        copy.start()
        copies.append(copy)
    for copy in copies:
        copy.wait()


def weight_kernel(
    mine_in, other_in, mine_rows, share_out, first_out, second_out, third_out,
    mine_ref, other_ref, rows_ref, share_ref, parts_ref, load_sem, store_sem,
):
    half = mine_ref.shape[1]
    middle = half // 2 // LANES * LANES
    upper, lower = slice(middle, half), slice(0, middle)
    loads = []
    for source, target, here in (
        (mine_in, mine_ref, upper),
        (other_in, other_ref, slice(half, None)),
        (other_in, other_ref, upper),
        (mine_in, mine_ref, lower),
        (other_in, other_ref, lower),
    ):
        load = pltpu.make_async_copy(
            source.at[:, here], target.at[:, here], load_sem.at[len(loads)]
        )
        load.start()
        loads.append(load)
    assemble(mine_rows, rows_ref)
    block = share_ref.shape[0]
    stores = []
    for i, (k, out) in enumerate(
        ((2, second_out), (3, third_out), (1, first_out), (0, share_out))
    ):
        here = slice(k * block, (k + 1) * block)
        if i in (0, 2):
            loads[3 * (i // 2)].wait()
        grads = dot(mine_ref[:, here], rows_ref[...], TN)
        if i == 0:
            loads[1].wait()
            loads[2].wait()
        if i == 2:
            loads[4].wait()
        grads += dot(other_ref[:, here], other_ref[:, half:], TN)
        if k == 0:
            share_ref[...] = grads
            held = share_ref
        else:
            held = parts_ref.at[k - 1]
            held[...] = grads.astype(BF)
        store = pltpu.make_async_copy(held, out, store_sem.at[i])
        store.start()
        stores.append(store)
    for store in stores:
        store.wait()


def combine_kernel(
    scale, got_ref, pick_in, share_in, first_ref, second_ref, third_ref,
    grad_ref, loss_ref, weight_ref, pick_ref, share_ref, sem,
):
    clusters = got_ref.shape[0]
    width = grad_ref.shape[1]
    rows = grad_ref.shape[0]
    loads = [pltpu.make_async_copy(pick_in, pick_ref, sem.at[0])]
    loads.append(pltpu.make_async_copy(share_in, share_ref, sem.at[1]))
    for load in loads:
        load.start()
    loads[0].wait()
    pick = pick_ref[...].reshape(clusters, 2 * HALF, rows)
    pick_a = pick[:, :HALF].reshape(clusters * HALF, rows)
    pick_b = pick[:, HALF:].reshape(clusters * HALF, rows)

    def lanes(start, size):
        return got_ref[:, :, start : start + size].reshape(clusters * HALF, size)

    grads = dot(pick_a, lanes(0, width), TN) + dot(pick_b, lanes(width, width), TN)
    grad_ref[...] = grads.astype(BF)
    terms = lanes(2 * width, LANES)
    first = dot(terms, pick_a, TN)
    second = dot(terms, pick_b, TN)
    loss = jnp.sum(first[:4], axis=0, keepdims=True) + jnp.sum(second[4:8], axis=0, keepdims=True)
    loss_ref[...] = loss * scale
    loads[1].wait()
    total = share_ref[...]
    for part in (first_ref, second_ref, third_ref):
        total += part[...].astype(F32)
    weight_ref[...] = total[: weight_ref.shape[0]].astype(BF)


def whole(shape, dtype):
    return jax.ShapeDtypeStruct(shape, dtype)


VM = pl.BlockSpec(memory_space=pltpu.VMEM)
SM = pl.BlockSpec(memory_space=pltpu.SMEM)
HBM = pl.BlockSpec(memory_space=pltpu.HBM)


def in_hbm(array):
    return pltpu.with_memory_space_constraint(array, pltpu.HBM)


PARAMS = pltpu.CompilerParams(vmem_limit_bytes=VMEM_LIMIT)


def local(embed, weights, shortlist, positives):
    rows, width = embed.shape
    slots_k = shortlist.shape[1]
    count = positives.shape[1]
    _, labels, _ = weights.shape
    clusters = lax.axis_size("clus")
    shards = lax.axis_size("rows")
    wide = 2 * width + LANES
    total = clusters * 2 * HALF
    block = labels // shards
    tall = padded(block)
    half = shards // 2

    place = lax.axis_index("rows")
    core, x = place % 2, place // 2
    order = [((x + k) % half) * 2 + side for side in (1 - core, core) for k in range(half)]

    send, pick = pl.pallas_call(
        functools.partial(pack_kernel, labels, shards),
        out_shape=(whole((clusters, HALF, wide), BF), whole((total, rows), BF)),
        in_specs=[VM] * 3,
        out_specs=(VM, VM),
        compiler_params=pltpu.CompilerParams(vmem_limit_bytes=60 * 1024 * 1024),
    )(embed, shortlist.T, positives.T)
    recv = lax.all_to_all(send, "clus", 0, 0, tiled=True)

    table = jnp.pad(weights.reshape(shards, block, width), ((0, 0), (0, tall - block), (0, 0)))
    table = jnp.stack([lax.dynamic_index_in_dim(table, k, 0, keepdims=False) for k in order])
    table = table.reshape(shards * tall, width)
    column = np.arange(shards * tall)
    pads = np.bincount(column[column % tall >= block] % LANES, minlength=LANES)
    pads = np.stack([pads, 0.5**pads]).astype(np.float32)
    back, give, keep = pl.pallas_call(
        functools.partial(score_kernel, count),
        out_shape=(
            pltpu.HBM((clusters, HALF, wide), BF),
            pltpu.HBM((total, half * tall + width), BF),
            pltpu.HBM((total, half * tall), BF),
        ),
        in_specs=[VM, HBM, VM],
        out_specs=(HBM, HBM, HBM),
        scratch_shapes=[
            pltpu.VMEM((shards * tall, width), BF),
            pltpu.VMEM((clusters, HALF, wide), BF),
            pltpu.VMEM((total, width), BF),
            pltpu.VMEM((total, LANES), jnp.int32),
            pltpu.VMEM((2, total, CHUNK), F32),
            pltpu.VMEM((total, shards * tall), BF),
            pltpu.VMEM((total, LANES), F32),
            pltpu.VMEM((total, LANES), F32),
            pltpu.VMEM((total, LANES), F32),
            pltpu.SemaphoreType.DMA((shards * tall // CHUNK,)),
            pltpu.SemaphoreType.DMA((2 * total // BLOCK,)),
            pltpu.SemaphoreType.DMA((total // BLOCK,)),
            pltpu.SemaphoreType.DMA,
        ],
        compiler_params=PARAMS,
    )(recv, in_hbm(table), jnp.asarray(pads))
    got = lax.all_to_all(back, "clus", 0, 0, tiled=True)

    swap = [(i, i ^ 1) for i in range(shards)]
    other = lax.ppermute(give, "rows", swap)
    share, *pieces = pl.pallas_call(
        weight_kernel,
        out_shape=(pltpu.HBM((tall, width), F32),) + (pltpu.HBM((tall, width), BF),) * 3,
        in_specs=[HBM, HBM, VM],
        out_specs=(HBM,) * 4,
        scratch_shapes=[
            pltpu.VMEM((total, half * tall), BF),
            pltpu.VMEM((total, half * tall + width), BF),
            pltpu.VMEM((total, width), BF),
            pltpu.VMEM((tall, width), F32),
            pltpu.VMEM((half - 1, tall, width), BF),
            pltpu.SemaphoreType.DMA((5,)),
            pltpu.SemaphoreType.DMA((4,)),
        ],
        compiler_params=PARAMS,
        cost_estimate=pl.CostEstimate(flops=1, bytes_accessed=1, transcendentals=0),
    )(in_hbm(keep), in_hbm(other), recv)
    arrived = []
    for k in (2, 1, 3):
        perm = [(i, (i + 2 * k) % shards) for i in range(shards)]
        arrived.append(lax.ppermute(pieces[k - 1], "rows", perm))

    row_grad, row_loss, weight_grad = pl.pallas_call(
        functools.partial(combine_kernel, 1.0 / (slots_k * labels)),
        out_shape=(whole((rows, width), BF), whole((1, rows), F32), whole((block, width), BF)),
        in_specs=[VM, HBM, HBM, VM, VM, VM],
        out_specs=(VM, VM, VM),
        scratch_shapes=[
            pltpu.VMEM((total, rows), BF),
            pltpu.VMEM((tall, width), F32),
            pltpu.SemaphoreType.DMA((2,)),
        ],
        compiler_params=PARAMS,
    )(got, in_hbm(pick), in_hbm(share), *arrived)
    return row_grad, row_loss.reshape(rows), weight_grad[None]


def solution(mesh):
    placed = (
        P(("rows", "clus"), None),
        P("clus", None, None),
        P(("rows", "clus"), None),
        P(("rows", "clus"), None),
    )
    return jax.shard_map(
        local,
        mesh=mesh,
        in_specs=placed,
        out_specs=(P(("rows", "clus"), None), P(("rows", "clus")), P("clus", "rows", None)),
        check_vma=False,
    )
```

```python
import functools
import jax
import jax.numpy as jnp
import numpy as np
from jax import lax
from jax.experimental import pallas as pl
from jax.experimental.pallas import tpu as pltpu
from jax.sharding import PartitionSpec as P

BF = jnp.bfloat16
F32 = jnp.float32
LANES = 128
CHUNK = 256
CAP = 32
GROUP = 8
GROUP_LANES = 32
VMEM_LIMIT = 40 * 1024 * 1024
TALL = 32
BLOCK = 512
LOG2E = 1.4426950408889634

NT = (((1,), (1,)), ((), ()))
TN = (((0,), (0,)), ((), ()))
NN = (((1,), (0,)), ((), ()))


def dot(a, b, dims=NN):
    return lax.dot_general(a, b, dims, preferred_element_type=F32)


def iota(shape, dim):
    return lax.broadcasted_iota(jnp.int32, shape, dim)


def padded(block):
    return -(-block // 32) * 32


def pack_kernel(
    labels, shards, embed_ref, short_ref, pos_ref, send_out, pick_ref, held_ref, sem
):
    rows, width = embed_ref.shape
    slots_k = short_ref.shape[0]
    clusters = send_out.shape[0]
    cap = CAP
    block = labels // shards
    place = lax.axis_index("rows")
    core, x = lax.rem(place, 2), lax.div(place, 2)
    half = shards // 2
    shift = []
    for b in range(shards):
        step = lax.rem(b // 2 - x + half, half)
        slot = step + jnp.where(core == b % 2, half, 0)
        shift.append(padded(block) * slot - block * b)
    short = short_ref[...]
    pos = pos_ref[...]
    count = pos.shape[0]
    cluster_id = iota((clusters, rows), 0)
    member = jnp.zeros((clusters, rows), F32)
    for j in range(slots_k):
        member += (short[j : j + 1, :] == cluster_id).astype(F32)
    before = (iota((rows, rows), 0) < iota((rows, rows), 1)).astype(BF)
    rank = dot(member.astype(BF), before)
    code = jnp.where(member > 0.5, rank, -1.0)
    slot = iota((clusters, cap, rows), 1).astype(F32)
    pick = (code[:, None, :] == slot).astype(F32)
    pick = pick.reshape(clusters * cap, rows).astype(BF)
    pick_ref[...] = pick
    values, names = [], []
    for j in range(slots_k):
        local = pos - j * labels
        inside = jnp.logical_and(local >= 0, local < labels)
        column = local + shift[0]
        for b in range(1, shards):
            column += jnp.where(local >= b * block, shift[b] - shift[b - 1], 0)
        column = jnp.where(inside, column, 0)
        bit = lax.shift_left(jnp.ones_like(column), lax.shift_right_logical(column, 7))
        values.append(jnp.where(inside, bit, 0).astype(F32))
        values.append(jnp.bitwise_and(column, LANES - 1).astype(F32))
        names.append(jnp.broadcast_to(short[j : j + 1, :], (2 * count, rows)).astype(F32))
    used = 2 * count * slots_k
    rest = jnp.zeros((LANES - used, rows), F32)
    values = jnp.concatenate(values + [rest], axis=0).astype(BF)
    names = jnp.concatenate(names + [rest], axis=0).astype(BF)
    got_values = dot(pick, values, NT)
    got_names = dot(pick, names, NT)
    own = lax.shift_right_logical(iota(got_values.shape, 0), 5).astype(F32)
    kept = jnp.where(got_names == own, got_values, 0.0)
    kept = kept.reshape(clusters, cap // GROUP, GROUP, LANES)
    source = iota((LANES, LANES), 0)
    folded = jnp.bitwise_and(source, 2 * count - 1)
    folded = jnp.where(source < used, folded, LANES)
    target = iota((LANES, LANES), 1)
    meta = jnp.zeros((clusters * GROUP, LANES), F32)
    for g in range(cap // GROUP):
        fold = (folded + g * GROUP_LANES == target).astype(BF)
        part = kept[:, g].reshape(clusters * GROUP, LANES).astype(BF)
        meta += dot(part, fold)
    held_ref[:, width // LANES * cap :, :] = meta.astype(BF).reshape(clusters, GROUP, LANES)
    step = clusters // 4
    copies = []
    for i in range(4):
        here = slice(i * step, (i + 1) * step)
        got = dot(pick[i * step * cap : (i + 1) * step * cap], embed_ref[...]).astype(BF)
        for k in range(width // LANES):
            part = got[:, k * LANES : (k + 1) * LANES]
            held_ref[here, k * cap : (k + 1) * cap, :] = part.reshape(step, cap, LANES)
        copy = pltpu.make_async_copy(held_ref.at[here], send_out.at[here], sem.at[i])
        copy.start()
        copies.append(copy)
    for copy in copies:
        copy.wait()


def assemble(recv_ref, rows_ref):
    total, width = rows_ref.shape
    for k in range(width // LANES):
        part = recv_ref[:, k * CAP : (k + 1) * CAP, :]
        rows_ref[:, k * LANES : (k + 1) * LANES] = part.reshape(total, LANES)


def target_bits(count, recv_ref, bits_ref, width):
    sources = recv_ref.shape[0]
    step = 8
    tall = step * GROUP
    for start in range(0, sources, step):
        meta = recv_ref[start : start + step, width // LANES * CAP :, :]
        meta = meta.astype(F32).astype(jnp.int32).reshape(tall, LANES)
        lane = iota((tall, LANES), 1)
        groups = []
        for g in range(CAP // GROUP):
            base = g * GROUP_LANES
            bits = jnp.zeros((tall, LANES), jnp.int32)
            for p in range(count):
                value = meta[:, base + p : base + p + 1]
                place = meta[:, base + count + p : base + count + p + 1]
                bits = jnp.bitwise_or(bits, jnp.where(place == lane, value, 0))
            groups.append(bits.reshape(step, GROUP, LANES))
        both = jnp.concatenate(groups, axis=1)
        bits_ref[start * CAP : (start + step) * CAP] = both.reshape(step * CAP, LANES)


def score_kernel(
    count, recv_ref, table_ref, pads_ref, back_out, give_out, keep_out,
    weight_ref, back_ref, rows_ref, bits_ref, s_ref, error_ref, relu_ref, prod_ref, sum_ref,
    weight_sem, error_sem, back_sem, rows_sem,
):
    sources = recv_ref.shape[0]
    total, width = rows_ref.shape
    chunks = weight_ref.shape[0] // CHUNK
    loads = []
    for i in range(chunks):
        here = slice(i * CHUNK, (i + 1) * CHUNK)
        load = pltpu.make_async_copy(table_ref.at[here], weight_ref.at[here], weight_sem.at[i])
        load.start()
        loads.append(load)
    assemble(recv_ref, rows_ref)
    spare = pltpu.make_async_copy(rows_ref, give_out.at[:, keep_out.shape[1] :], rows_sem)
    spare.start()
    target_bits(count, recv_ref, bits_ref, width)
    copies = [spare]

    def score(i, at):
        chunk = weight_ref[i * CHUNK : (i + 1) * CHUNK]
        s_ref[i % 2, at] = dot(rows_ref[at], chunk, NT)

    def pointwise(i, at):
        for start in range(at.start, at.stop, TALL):
            here = slice(start, start + TALL)
            bits = bits_ref[here]
            if i == 0:
                relu = jnp.zeros((TALL, LANES), F32)
                prod = jnp.ones((TALL, LANES), F32)
                summed = relu
            else:
                relu, prod, summed = relu_ref[here], prod_ref[here], sum_ref[here]
            for part in range(CHUNK // LANES):
                column = i * CHUNK + part * LANES
                s = s_ref[i % 2, here, part * LANES : (part + 1) * LANES]
                hit = lax.shift_left(bits, 31 - column // LANES) < 0
                size = jnp.abs(s)
                e = jnp.exp2(size * -LOG2E)
                d = 1.0 + e
                r = pl.reciprocal(d, approx=True)
                up = jnp.logical_xor(s >= 0.0, hit)
                chance = jnp.where(up, r, e * r)
                error = jnp.where(hit, -chance, chance)
                error_ref[here, column : column + LANES] = error.astype(BF)
                relu = relu + jnp.where(up, size, 0.0)
                prod = prod * d
                summed = summed + e
            relu_ref[here] = relu
            prod_ref[here] = prod
            sum_ref[here] = summed

    def flush(at):
        half = keep_out.shape[1]
        for k, out in enumerate((give_out, keep_out)):
            copy = pltpu.make_async_copy(
                error_ref.at[at, k * half : (k + 1) * half],
                out.at[at, :half],
                error_sem.at[2 * (at.start // BLOCK) + k],
            )
            copy.start()
            copies.append(copy)

    blocks = [slice(k, k + BLOCK) for k in range(0, total, BLOCK)]
    for i in range(-1, chunks):
        if i + 1 < chunks:
            loads[i + 1].wait()
        for at in blocks:
            if i + 1 < chunks:
                score(i + 1, at)
            if i >= 0:
                pointwise(i, at)
    for at in blocks:
        flush(at)

    summed = sum_ref[...] - pads_ref[0:1]
    tail = jnp.where(summed < 4e-4, summed, jnp.log(prod_ref[...] * pads_ref[1:2]))
    loss = jnp.sum(relu_ref[...] + tail, axis=1, keepdims=True)
    first = loss.astype(BF).astype(F32)
    second = (loss - first).astype(BF).astype(F32)
    third = loss - first - second
    part = jnp.bitwise_and(iota((total, LANES), 1), 3)
    terms = jnp.where(part == 2, third, 0.0)
    terms = jnp.where(part == 1, second, terms)
    terms = jnp.where(part == 0, first, terms)
    terms = terms.reshape(sources, CAP // GROUP, GROUP, LANES)
    group = lax.shift_right_logical(iota((sources, GROUP, LANES), 2), 2)
    mixed = jnp.zeros((sources, GROUP, LANES), F32)
    for g in range(CAP // GROUP):
        mixed = jnp.where(group == g, terms[:, g], mixed)
    back_ref[:, width // LANES * CAP :, :] = mixed.astype(BF)
    for at in blocks:
        first, last = at.start // CAP, at.stop // CAP
        grads = dot(error_ref[at], weight_ref[...]).astype(BF)
        for k in range(width // LANES):
            part = grads[:, k * LANES : (k + 1) * LANES]
            back_ref[first:last, k * CAP : (k + 1) * CAP, :] = part.reshape(last - first, CAP, LANES)
        copy = pltpu.make_async_copy(
            back_ref.at[first:last], back_out.at[first:last], back_sem.at[at.start // BLOCK]
        )
        copy.start()
        copies.append(copy)
    for copy in copies:
        copy.wait()


def weight_kernel(
    mine_in, other_in, mine_rows, share_out, first_out, second_out, third_out,
    mine_ref, other_ref, rows_ref, share_ref, parts_ref, load_sem, store_sem,
):
    half = mine_ref.shape[1]
    middle = half // 2 // LANES * LANES
    upper, lower = slice(middle, half), slice(0, middle)
    loads = []
    for source, target, here in (
        (mine_in, mine_ref, upper),
        (other_in, other_ref, slice(half, None)),
        (other_in, other_ref, upper),
        (mine_in, mine_ref, lower),
        (other_in, other_ref, lower),
    ):
        load = pltpu.make_async_copy(
            source.at[:, here], target.at[:, here], load_sem.at[len(loads)]
        )
        load.start()
        loads.append(load)
    assemble(mine_rows, rows_ref)
    block = share_ref.shape[0]
    stores = []
    for i, (k, out) in enumerate(
        ((2, second_out), (3, third_out), (1, first_out), (0, share_out))
    ):
        here = slice(k * block, (k + 1) * block)
        if i in (0, 2):
            loads[3 * (i // 2)].wait()
        grads = dot(mine_ref[:, here], rows_ref[...], TN)
        if i == 0:
            loads[1].wait()
            loads[2].wait()
        if i == 2:
            loads[4].wait()
        grads += dot(other_ref[:, here], other_ref[:, half:], TN)
        if k == 0:
            share_ref[...] = grads
            held = share_ref
        else:
            held = parts_ref.at[k - 1]
            held[...] = grads.astype(BF)
        store = pltpu.make_async_copy(held, out, store_sem.at[i])
        store.start()
        stores.append(store)
    for store in stores:
        store.wait()


def combine_kernel(
    scale, got_ref, pick_in, share_in, first_ref, second_ref, third_ref,
    grad_ref, loss_ref, weight_ref, pick_ref, share_ref, sem,
):
    clusters = got_ref.shape[0]
    width = grad_ref.shape[1]
    rows = grad_ref.shape[0]
    loads = [pltpu.make_async_copy(pick_in, pick_ref, sem.at[0])]
    loads.append(pltpu.make_async_copy(share_in, share_ref, sem.at[1]))
    for load in loads:
        load.start()
    loads[1].wait()
    summed = share_ref[...]
    for part in (first_ref, second_ref, third_ref):
        summed += part[...].astype(F32)
    weight_ref[...] = summed[: weight_ref.shape[0]].astype(BF)
    loads[0].wait()
    parts = []
    for k in range(width // LANES):
        part = got_ref[:, k * CAP : (k + 1) * CAP, :]
        parts.append(part.reshape(clusters * CAP, LANES))
    grads = dot(pick_ref[...], jnp.concatenate(parts, axis=1), TN)
    grad_ref[...] = grads.astype(BF)
    terms = got_ref[:, width // LANES * CAP :, :].reshape(clusters * GROUP, LANES)
    pick = pick_ref[...].astype(F32).reshape(clusters, CAP // GROUP, GROUP, rows)
    loss = jnp.zeros((1, rows), F32)
    for g in range(CAP // GROUP):
        chosen = pick[:, g].reshape(clusters * GROUP, rows).astype(BF)
        found = dot(terms, chosen, TN)
        loss += jnp.sum(found[4 * g : 4 * g + 4], axis=0, keepdims=True)
    loss_ref[...] = loss * scale


def whole(shape, dtype):
    return jax.ShapeDtypeStruct(shape, dtype)


VM = pl.BlockSpec(memory_space=pltpu.VMEM)
SM = pl.BlockSpec(memory_space=pltpu.SMEM)
HBM = pl.BlockSpec(memory_space=pltpu.HBM)


def in_hbm(array):
    return pltpu.with_memory_space_constraint(array, pltpu.HBM)


PARAMS = pltpu.CompilerParams(vmem_limit_bytes=VMEM_LIMIT)


def local(embed, weights, shortlist, positives):
    rows, width = embed.shape
    slots_k = shortlist.shape[1]
    count = positives.shape[1]
    _, labels, _ = weights.shape
    clusters = lax.axis_size("clus")
    shards = lax.axis_size("rows")
    shape = (clusters, width // LANES * CAP + GROUP, LANES)
    total = clusters * CAP
    block = labels // shards
    tall = padded(block)
    half = shards // 2

    place = lax.axis_index("rows")
    core, x = place % 2, place // 2
    order = [((x + k) % half) * 2 + side for side in (1 - core, core) for k in range(half)]

    send, pick = pl.pallas_call(
        functools.partial(pack_kernel, labels, shards),
        out_shape=(pltpu.HBM(shape, BF), whole((total, rows), BF)),
        in_specs=[VM] * 3,
        out_specs=(HBM, VM),
        scratch_shapes=[pltpu.VMEM(shape, BF), pltpu.SemaphoreType.DMA((4,))],
        compiler_params=pltpu.CompilerParams(vmem_limit_bytes=60 * 1024 * 1024),
    )(embed, shortlist.T, positives.T)
    recv = lax.all_to_all(send, "clus", 0, 0, tiled=True)

    table = jnp.pad(weights.reshape(shards, block, width), ((0, 0), (0, tall - block), (0, 0)))
    table = jnp.stack([lax.dynamic_index_in_dim(table, k, 0, keepdims=False) for k in order])
    table = table.reshape(shards * tall, width)
    column = np.arange(shards * tall)
    pads = np.bincount(column[column % tall >= block] % LANES, minlength=LANES)
    pads = np.stack([pads, 0.5**pads]).astype(np.float32)
    back, give, keep = pl.pallas_call(
        functools.partial(score_kernel, count),
        out_shape=(
            pltpu.HBM(shape, BF),
            pltpu.HBM((total, half * tall + width), BF),
            pltpu.HBM((total, half * tall), BF),
        ),
        in_specs=[VM, HBM, VM],
        out_specs=(HBM, HBM, HBM),
        scratch_shapes=[
            pltpu.VMEM((shards * tall, width), BF),
            pltpu.VMEM(shape, BF),
            pltpu.VMEM((total, width), BF),
            pltpu.VMEM((total, LANES), jnp.int32),
            pltpu.VMEM((2, total, CHUNK), F32),
            pltpu.VMEM((total, shards * tall), BF),
            pltpu.VMEM((total, LANES), F32),
            pltpu.VMEM((total, LANES), F32),
            pltpu.VMEM((total, LANES), F32),
            pltpu.SemaphoreType.DMA((shards * tall // CHUNK,)),
            pltpu.SemaphoreType.DMA((2 * total // BLOCK,)),
            pltpu.SemaphoreType.DMA((total // BLOCK,)),
            pltpu.SemaphoreType.DMA,
        ],
        compiler_params=PARAMS,
    )(recv, in_hbm(table), jnp.asarray(pads))
    got = lax.all_to_all(back, "clus", 0, 0, tiled=True)

    swap = [(i, i ^ 1) for i in range(shards)]
    other = lax.ppermute(give, "rows", swap)
    share, *pieces = pl.pallas_call(
        weight_kernel,
        out_shape=(pltpu.HBM((tall, width), F32),) + (pltpu.HBM((tall, width), BF),) * 3,
        in_specs=[HBM, HBM, VM],
        out_specs=(HBM,) * 4,
        scratch_shapes=[
            pltpu.VMEM((total, half * tall), BF),
            pltpu.VMEM((total, half * tall + width), BF),
            pltpu.VMEM((total, width), BF),
            pltpu.VMEM((tall, width), F32),
            pltpu.VMEM((half - 1, tall, width), BF),
            pltpu.SemaphoreType.DMA((5,)),
            pltpu.SemaphoreType.DMA((4,)),
        ],
        compiler_params=PARAMS,
        cost_estimate=pl.CostEstimate(flops=1, bytes_accessed=1, transcendentals=0),
    )(in_hbm(keep), in_hbm(other), recv)
    arrived = []
    for k in (2, 1, 3):
        perm = [(i, (i + 2 * k) % shards) for i in range(shards)]
        arrived.append(lax.ppermute(pieces[k - 1], "rows", perm))

    row_grad, row_loss, weight_grad = pl.pallas_call(
        functools.partial(combine_kernel, 1.0 / (slots_k * labels)),
        out_shape=(whole((rows, width), BF), whole((1, rows), F32), whole((block, width), BF)),
        in_specs=[VM, HBM, HBM, VM, VM, VM],
        out_specs=(VM, VM, VM),
        scratch_shapes=[
            pltpu.VMEM((total, rows), BF),
            pltpu.VMEM((tall, width), F32),
            pltpu.SemaphoreType.DMA((2,)),
        ],
        compiler_params=PARAMS,
    )(got, in_hbm(pick), in_hbm(share), *arrived)
    return row_grad, row_loss.reshape(rows), weight_grad[None]


def solution(mesh):
    placed = (
        P(("rows", "clus"), None),
        P("clus", None, None),
        P(("rows", "clus"), None),
        P(("rows", "clus"), None),
    )
    return jax.shard_map(
        local,
        mesh=mesh,
        in_specs=placed,
        out_specs=(P(("rows", "clus"), None), P(("rows", "clus")), P("clus", "rows", None)),
        check_vma=False,
    )
```

```python
import functools
import jax
import jax.numpy as jnp
import numpy as np
from jax import lax
from jax.experimental import pallas as pl
from jax.experimental.pallas import tpu as pltpu
from jax.sharding import PartitionSpec as P

BF = jnp.bfloat16
F32 = jnp.float32
LANES = 128
CHUNK = 256
CAP = 32
GROUP = 8
GROUP_LANES = 32
VMEM_LIMIT = 40 * 1024 * 1024
TALL = 32
BLOCK = 512
LOG2E = 1.4426950408889634

NT = (((1,), (1,)), ((), ()))
TN = (((0,), (0,)), ((), ()))
NN = (((1,), (0,)), ((), ()))


def dot(a, b, dims=NN):
    return lax.dot_general(a, b, dims, preferred_element_type=F32)


def iota(shape, dim):
    return lax.broadcasted_iota(jnp.int32, shape, dim)


def padded(block):
    return -(-block // 32) * 32


def pack_kernel(
    labels, shards, embed_ref, short_ref, pos_ref, send_ref, pick_ref
):
    rows, width = embed_ref.shape
    slots_k = short_ref.shape[0]
    clusters = send_ref.shape[0]
    cap = CAP
    block = labels // shards
    place = lax.axis_index("rows")
    core, x = lax.rem(place, 2), lax.div(place, 2)
    half = shards // 2
    shift = []
    for b in range(shards):
        step = lax.rem(b // 2 - x + half, half)
        slot = step + jnp.where(core == b % 2, half, 0)
        shift.append(padded(block) * slot - block * b)
    short = short_ref[...]
    pos = pos_ref[...]
    count = pos.shape[0]
    cluster_id = iota((clusters, rows), 0)
    member = jnp.zeros((clusters, rows), F32)
    for j in range(slots_k):
        member += (short[j : j + 1, :] == cluster_id).astype(F32)
    before = (iota((rows, rows), 0) < iota((rows, rows), 1)).astype(BF)
    rank = dot(member.astype(BF), before)
    code = jnp.where(member > 0.5, rank, -1.0)
    slot = iota((clusters, cap, rows), 1).astype(F32)
    pick = (code[:, None, :] == slot).astype(F32)
    pick = pick.reshape(clusters * cap, rows).astype(BF)
    pick_ref[...] = pick
    values, names = [], []
    for j in range(slots_k):
        local = pos - j * labels
        inside = jnp.logical_and(local >= 0, local < labels)
        column = local + shift[0]
        for b in range(1, shards):
            column += jnp.where(local >= b * block, shift[b] - shift[b - 1], 0)
        column = jnp.where(inside, column, 0)
        bit = lax.shift_left(jnp.ones_like(column), lax.shift_right_logical(column, 7))
        values.append(jnp.where(inside, bit, 0).astype(F32))
        values.append(jnp.bitwise_and(column, LANES - 1).astype(F32))
        names.append(jnp.broadcast_to(short[j : j + 1, :], (2 * count, rows)).astype(F32))
    used = 2 * count * slots_k
    rest = jnp.zeros((LANES - used, rows), F32)
    values = jnp.concatenate(values + [rest], axis=0).astype(BF)
    names = jnp.concatenate(names + [rest], axis=0).astype(BF)
    got_values = dot(pick, values, NT)
    got_names = dot(pick, names, NT)
    own = lax.shift_right_logical(iota(got_values.shape, 0), 5).astype(F32)
    kept = jnp.where(got_names == own, got_values, 0.0)
    source = iota((LANES, LANES), 0)
    target = iota((LANES, LANES), 1)
    match = jnp.bitwise_and(source, 2 * count - 1) == jnp.bitwise_and(target, GROUP_LANES - 1)
    fold = jnp.logical_and(source < used, match).astype(BF)
    found = dot(kept.astype(BF), fold).reshape(clusters, cap // GROUP, GROUP, LANES)
    group = iota((clusters, GROUP, LANES), 2) // GROUP_LANES
    meta = found[:, 0]
    for g in range(1, cap // GROUP):
        meta = jnp.where(group == g, found[:, g], meta)
    send_ref[:, width // LANES * cap :, :] = meta.astype(BF)
    got = dot(pick, embed_ref[...]).astype(BF)
    for k in range(width // LANES):
        part = got[:, k * LANES : (k + 1) * LANES]
        send_ref[:, k * cap : (k + 1) * cap, :] = part.reshape(clusters, cap, LANES)


def assemble(recv_ref, rows_ref):
    total, width = rows_ref.shape
    for k in range(width // LANES):
        part = recv_ref[:, k * CAP : (k + 1) * CAP, :]
        rows_ref[:, k * LANES : (k + 1) * LANES] = part.reshape(total, LANES)


def target_bits(count, recv_ref, bits_ref, width):
    sources = recv_ref.shape[0]
    step = 8
    tall = step * GROUP
    for start in range(0, sources, step):
        meta = recv_ref[start : start + step, width // LANES * CAP :, :]
        meta = meta.astype(F32).astype(jnp.int32).reshape(tall, LANES)
        lane = iota((tall, LANES), 1)
        groups = []
        for g in range(CAP // GROUP):
            base = g * GROUP_LANES
            bits = jnp.zeros((tall, LANES), jnp.int32)
            for p in range(count):
                value = meta[:, base + p : base + p + 1]
                place = meta[:, base + count + p : base + count + p + 1]
                bits = jnp.bitwise_or(bits, jnp.where(place == lane, value, 0))
            groups.append(bits.reshape(step, GROUP, LANES))
        both = jnp.concatenate(groups, axis=1)
        bits_ref[start * CAP : (start + step) * CAP] = both.reshape(step * CAP, LANES)


def score_kernel(
    count, recv_ref, table_ref, pads_ref, back_out, give_out, keep_out,
    weight_ref, back_ref, rows_ref, bits_ref, s_ref, error_ref, relu_ref, prod_ref, sum_ref,
    weight_sem, error_sem, back_sem, rows_sem,
):
    sources = recv_ref.shape[0]
    total, width = rows_ref.shape
    chunks = weight_ref.shape[0] // CHUNK
    loads = []
    for i in range(chunks):
        here = slice(i * CHUNK, (i + 1) * CHUNK)
        load = pltpu.make_async_copy(table_ref.at[here], weight_ref.at[here], weight_sem.at[i])
        load.start()
        loads.append(load)
    assemble(recv_ref, rows_ref)
    spare = pltpu.make_async_copy(rows_ref, give_out.at[:, keep_out.shape[1] :], rows_sem)
    spare.start()
    target_bits(count, recv_ref, bits_ref, width)
    copies = [spare]

    def score(i, at):
        chunk = weight_ref[i * CHUNK : (i + 1) * CHUNK]
        s_ref[i % 2, at] = dot(rows_ref[at], chunk, NT)

    def pointwise(i, at):
        for start in range(at.start, at.stop, TALL):
            here = slice(start, start + TALL)
            bits = bits_ref[here]
            if i == 0:
                relu = jnp.zeros((TALL, LANES), F32)
                prod = jnp.ones((TALL, LANES), F32)
                summed = relu
            else:
                relu, prod, summed = relu_ref[here], prod_ref[here], sum_ref[here]
            for part in range(CHUNK // LANES):
                column = i * CHUNK + part * LANES
                s = s_ref[i % 2, here, part * LANES : (part + 1) * LANES]
                hit = lax.shift_left(bits, 31 - column // LANES) < 0
                size = jnp.abs(s)
                e = jnp.exp2(size * -LOG2E)
                d = 1.0 + e
                r = pl.reciprocal(d, approx=True)
                up = jnp.logical_xor(s >= 0.0, hit)
                chance = jnp.where(up, r, e * r)
                error = jnp.where(hit, -chance, chance)
                error_ref[here, column : column + LANES] = error.astype(BF)
                relu = relu + jnp.where(up, size, 0.0)
                prod = prod * d
                summed = summed + e
            relu_ref[here] = relu
            prod_ref[here] = prod
            sum_ref[here] = summed

    def flush(at):
        half = keep_out.shape[1]
        for k, out in enumerate((give_out, keep_out)):
            copy = pltpu.make_async_copy(
                error_ref.at[at, k * half : (k + 1) * half],
                out.at[at, :half],
                error_sem.at[2 * (at.start // BLOCK) + k],
            )
            copy.start()
            copies.append(copy)

    blocks = [slice(k, k + BLOCK) for k in range(0, total, BLOCK)]
    for i in range(-1, chunks):
        if i + 1 < chunks:
            loads[i + 1].wait()
        for at in blocks:
            if i + 1 < chunks:
                score(i + 1, at)
            if i >= 0:
                pointwise(i, at)
    for at in blocks:
        flush(at)

    summed = sum_ref[...] - pads_ref[0:1]
    tail = jnp.where(summed < 4e-4, summed, jnp.log(prod_ref[...] * pads_ref[1:2]))
    loss = jnp.sum(relu_ref[...] + tail, axis=1, keepdims=True)
    first = loss.astype(BF).astype(F32)
    second = (loss - first).astype(BF).astype(F32)
    third = loss - first - second
    part = jnp.bitwise_and(iota((total, LANES), 1), 3)
    terms = jnp.where(part == 2, third, 0.0)
    terms = jnp.where(part == 1, second, terms)
    terms = jnp.where(part == 0, first, terms)
    terms = terms.reshape(sources, CAP // GROUP, GROUP, LANES)
    group = lax.shift_right_logical(iota((sources, GROUP, LANES), 2), 2)
    mixed = jnp.zeros((sources, GROUP, LANES), F32)
    for g in range(CAP // GROUP):
        mixed = jnp.where(group == g, terms[:, g], mixed)
    back_ref[:, width // LANES * CAP :, :] = mixed.astype(BF)
    for at in blocks:
        first, last = at.start // CAP, at.stop // CAP
        grads = dot(error_ref[at], weight_ref[...]).astype(BF)
        for k in range(width // LANES):
            part = grads[:, k * LANES : (k + 1) * LANES]
            back_ref[first:last, k * CAP : (k + 1) * CAP, :] = part.reshape(last - first, CAP, LANES)
        copy = pltpu.make_async_copy(
            back_ref.at[first:last], back_out.at[first:last], back_sem.at[at.start // BLOCK]
        )
        copy.start()
        copies.append(copy)
    for copy in copies:
        copy.wait()


def weight_kernel(blocks, mine_in, other_in, mine_rows, *rest):
    outs, scratch = rest[: len(blocks)], rest[len(blocks) :]
    mine_ref, other_ref, partner_ref, rows_ref, held_ref, load_sem, store_sem = scratch
    half = mine_in.shape[1]
    block, width = outs[0].shape
    first = min(blocks) * block // LANES * LANES
    last = -(-(max(blocks) + 1) * block // LANES) * LANES
    here = slice(first, last)
    loads = []
    for source, target in (
        (mine_in.at[:, here], mine_ref),
        (other_in.at[:, half:], partner_ref),
        (other_in.at[:, here], other_ref),
    ):
        load = pltpu.make_async_copy(source, target, load_sem.at[len(loads)])
        load.start()
        loads.append(load)
    assemble(mine_rows, rows_ref)
    stores = []
    for i, k in enumerate(blocks):
        at = slice(k * block - first, (k + 1) * block - first)
        if i == 0:
            loads[0].wait()
        grads = dot(mine_ref[:, at], rows_ref[...], TN)
        if i == 0:
            loads[1].wait()
            loads[2].wait()
        grads += dot(other_ref[:, at], partner_ref[...], TN)
        held_ref[i] = grads.astype(held_ref.dtype)
        store = pltpu.make_async_copy(held_ref.at[i], outs[i], store_sem.at[i])
        store.start()
        stores.append(store)
    for store in stores:
        store.wait()


def combine_kernel(
    scale, got_ref, pick_in, share_in, first_in, second_in, third_in,
    grad_out, loss_ref, weight_ref, pick_ref, share_ref, parts_ref, grad_ref, sem,
):
    clusters = got_ref.shape[0]
    rows, width = grad_ref.shape
    loads = [pltpu.make_async_copy(pick_in, pick_ref, sem.at[0])]
    loads.append(pltpu.make_async_copy(share_in, share_ref, sem.at[1]))
    for k, part in enumerate((first_in, second_in, third_in)):
        loads.append(pltpu.make_async_copy(part, parts_ref.at[k], sem.at[2 + k]))
    for load in loads:
        load.start()
    parts = []
    for k in range(width // LANES):
        part = got_ref[:, k * CAP : (k + 1) * CAP, :]
        parts.append(part.reshape(clusters * CAP, LANES))
    terms = got_ref[:, width // LANES * CAP :, :].astype(F32)
    group = lax.shift_right_logical(iota((clusters, GROUP, LANES), 2), 2)
    spread = [jnp.where(group == g, terms, 0.0) for g in range(CAP // GROUP)]
    parts.append(jnp.stack(spread, axis=1).reshape(clusters * CAP, LANES).astype(BF))
    loads[0].wait()
    summed = dot(pick_ref[...], jnp.concatenate(parts, axis=1), TN)
    grad_ref[...] = summed[:, :width].astype(BF)
    store = pltpu.make_async_copy(grad_ref, grad_out, sem.at[len(loads)])
    store.start()
    loss_ref[...] = jnp.sum(summed[:, width:].T, axis=0, keepdims=True) * scale
    for load in loads[1:]:
        load.wait()
    share = share_ref[...]
    for k in range(parts_ref.shape[0]):
        share += parts_ref[k].astype(F32)
    weight_ref[...] = share[: weight_ref.shape[0]].astype(BF)
    store.wait()


def whole(shape, dtype):
    return jax.ShapeDtypeStruct(shape, dtype)


VM = pl.BlockSpec(memory_space=pltpu.VMEM)
SM = pl.BlockSpec(memory_space=pltpu.SMEM)
HBM = pl.BlockSpec(memory_space=pltpu.HBM)


def in_hbm(array):
    return pltpu.with_memory_space_constraint(array, pltpu.HBM)


PARAMS = pltpu.CompilerParams(vmem_limit_bytes=VMEM_LIMIT)


def local(embed, weights, shortlist, positives):
    rows, width = embed.shape
    slots_k = shortlist.shape[1]
    count = positives.shape[1]
    _, labels, _ = weights.shape
    clusters = lax.axis_size("clus")
    shards = lax.axis_size("rows")
    shape = (clusters, width // LANES * CAP + GROUP, LANES)
    total = clusters * CAP
    block = labels // shards
    tall = padded(block)
    half = shards // 2

    place = lax.axis_index("rows")
    core, x = place % 2, place // 2
    order = [((x + k) % half) * 2 + side for side in (1 - core, core) for k in range(half)]

    send, pick = pl.pallas_call(
        functools.partial(pack_kernel, labels, shards),
        out_shape=(whole(shape, BF), whole((total, rows), BF)),
        in_specs=[VM] * 3,
        out_specs=(VM, VM),
        compiler_params=pltpu.CompilerParams(vmem_limit_bytes=60 * 1024 * 1024),
    )(embed, shortlist.T, positives.T)
    recv = lax.all_to_all(send, "clus", 0, 0, tiled=True)

    table = jnp.pad(weights.reshape(shards, block, width), ((0, 0), (0, tall - block), (0, 0)))
    table = jnp.stack([lax.dynamic_index_in_dim(table, k, 0, keepdims=False) for k in order])
    table = table.reshape(shards * tall, width)
    column = np.arange(shards * tall)
    pads = np.bincount(column[column % tall >= block] % LANES, minlength=LANES)
    pads = np.stack([pads, 0.5**pads]).astype(np.float32)
    back, give, keep = pl.pallas_call(
        functools.partial(score_kernel, count),
        out_shape=(
            pltpu.HBM(shape, BF),
            pltpu.HBM((total, half * tall + width), BF),
            pltpu.HBM((total, half * tall), BF),
        ),
        in_specs=[VM, HBM, VM],
        out_specs=(HBM, HBM, HBM),
        scratch_shapes=[
            pltpu.VMEM((shards * tall, width), BF),
            pltpu.VMEM(shape, BF),
            pltpu.VMEM((total, width), BF),
            pltpu.VMEM((total, LANES), jnp.int32),
            pltpu.VMEM((2, total, CHUNK), F32),
            pltpu.VMEM((total, shards * tall), BF),
            pltpu.VMEM((total, LANES), F32),
            pltpu.VMEM((total, LANES), F32),
            pltpu.VMEM((total, LANES), F32),
            pltpu.SemaphoreType.DMA((shards * tall // CHUNK,)),
            pltpu.SemaphoreType.DMA((2 * total // BLOCK,)),
            pltpu.SemaphoreType.DMA((total // BLOCK,)),
            pltpu.SemaphoreType.DMA,
        ],
        compiler_params=PARAMS,
    )(recv, in_hbm(table), jnp.asarray(pads))
    got = lax.all_to_all(back, "clus", 0, 0, tiled=True)

    swap = [(i, i ^ 1) for i in range(shards)]
    other = lax.ppermute(give, "rows", swap)
    def weight_part(blocks, dtype):
        first = min(blocks) * tall // LANES * LANES
        size = -(-(max(blocks) + 1) * tall // LANES) * LANES - first
        return pl.pallas_call(
            functools.partial(weight_kernel, blocks),
            out_shape=(pltpu.HBM((tall, width), dtype),) * len(blocks),
            in_specs=[HBM, HBM, VM],
            out_specs=(HBM,) * len(blocks),
            scratch_shapes=[
                pltpu.VMEM((total, size), BF),
                pltpu.VMEM((total, size), BF),
                pltpu.VMEM((total, width), BF),
                pltpu.VMEM((total, width), BF),
                pltpu.VMEM((len(blocks), tall, width), dtype),
                pltpu.SemaphoreType.DMA((3,)),
                pltpu.SemaphoreType.DMA((len(blocks),)),
            ],
            compiler_params=pltpu.CompilerParams(vmem_limit_bytes=20 * 1024 * 1024),
            cost_estimate=pl.CostEstimate(flops=1, bytes_accessed=1, transcendentals=0),
        )(in_hbm(keep), in_hbm(other), recv)

    away = tuple(range(1, half))
    arrived = []
    for k, piece in zip(away, weight_part(away, BF)):
        perm = [(i, (i + 2 * k) % shards) for i in range(shards)]
        arrived.append(lax.ppermute(piece, "rows", perm))
    (share,) = weight_part((0,), F32)
    row_grad, row_loss, weight_grad = pl.pallas_call(
        functools.partial(combine_kernel, 1.0 / (slots_k * labels)),
        out_shape=(
            pltpu.HBM((rows, width), BF),
            whole((1, rows), F32),
            whole((block, width), BF),
        ),
        in_specs=[VM] + [HBM] * 5,
        out_specs=(HBM, VM, VM),
        scratch_shapes=[
            pltpu.VMEM((total, rows), BF),
            pltpu.VMEM((tall, width), F32),
            pltpu.VMEM((half - 1, tall, width), BF),
            pltpu.VMEM((rows, width), BF),
            pltpu.SemaphoreType.DMA((6,)),
        ],
        compiler_params=pltpu.CompilerParams(vmem_limit_bytes=24 * 1024 * 1024),
    )(got, in_hbm(pick), in_hbm(share), *[in_hbm(part) for part in arrived])
    return row_grad, row_loss.reshape(rows), weight_grad[None]


def solution(mesh):
    placed = (
        P(("rows", "clus"), None),
        P("clus", None, None),
        P(("rows", "clus"), None),
        P(("rows", "clus"), None),
    )
    return jax.shard_map(
        local,
        mesh=mesh,
        in_specs=placed,
        out_specs=(P(("rows", "clus"), None), P(("rows", "clus")), P("clus", "rows", None)),
        check_vma=False,
    )
```

```python
import functools
import jax
import jax.numpy as jnp
import numpy as np
from jax import lax
from jax.experimental import pallas as pl
from jax.experimental.pallas import tpu as pltpu
from jax.sharding import PartitionSpec as P

BF = jnp.bfloat16
F32 = jnp.float32
LANES = 128
CHUNK = 256
CAP = 32
GROUP = 8
GROUP_LANES = 32
VMEM_LIMIT = 40 * 1024 * 1024
TALL = 16
BLOCK = 512
LOG2E = 1.4426950408889634

NT = (((1,), (1,)), ((), ()))
TN = (((0,), (0,)), ((), ()))
NN = (((1,), (0,)), ((), ()))


def dot(a, b, dims=NN):
    return lax.dot_general(a, b, dims, preferred_element_type=F32)


def iota(shape, dim):
    return lax.broadcasted_iota(jnp.int32, shape, dim)


def padded(block):
    return -(-block // 32) * 32


def pack_kernel(
    labels, shards, embed_ref, short_ref, pos_ref, send_ref, pick_ref
):
    rows, width = embed_ref.shape
    slots_k = short_ref.shape[0]
    clusters = send_ref.shape[0]
    cap = CAP
    block = labels // shards
    place = lax.axis_index("rows")
    core, x = lax.rem(place, 2), lax.div(place, 2)
    half = shards // 2
    shift = []
    for b in range(shards):
        step = lax.rem(b // 2 - x + half, half)
        slot = step + jnp.where(core == b % 2, half, 0)
        shift.append(padded(block) * slot - block * b)
    short = short_ref[...]
    pos = pos_ref[...]
    count = pos.shape[0]
    cluster_id = iota((clusters, rows), 0)
    member = jnp.zeros((clusters, rows), F32)
    for j in range(slots_k):
        member += (short[j : j + 1, :] == cluster_id).astype(F32)
    before = (iota((rows, rows), 0) < iota((rows, rows), 1)).astype(BF)
    rank = dot(member.astype(BF), before)
    code = jnp.where(member > 0.5, rank, -1.0)
    slot = iota((clusters, cap, rows), 1).astype(F32)
    pick = (code[:, None, :] == slot).astype(F32)
    pick = pick.reshape(clusters * cap, rows).astype(BF)
    pick_ref[...] = pick
    values, names = [], []
    for j in range(slots_k):
        local = pos - j * labels
        inside = jnp.logical_and(local >= 0, local < labels)
        column = local + shift[0]
        for b in range(1, shards):
            column += jnp.where(local >= b * block, shift[b] - shift[b - 1], 0)
        column = jnp.where(inside, column, 0)
        bit = lax.shift_left(jnp.ones_like(column), lax.shift_right_logical(column, 7))
        values.append(jnp.where(inside, bit, 0).astype(F32))
        values.append(jnp.bitwise_and(column, LANES - 1).astype(F32))
        names.append(jnp.broadcast_to(short[j : j + 1, :], (2 * count, rows)).astype(F32))
    used = 2 * count * slots_k
    rest = jnp.zeros((LANES - used, rows), F32)
    values = jnp.concatenate(values + [rest], axis=0).astype(BF)
    names = jnp.concatenate(names + [rest], axis=0).astype(BF)
    got_values = dot(pick, values, NT)
    got_names = dot(pick, names, NT)
    own = lax.shift_right_logical(iota(got_values.shape, 0), 5).astype(F32)
    kept = jnp.where(got_names == own, got_values, 0.0)
    source = iota((LANES, LANES), 0)
    target = iota((LANES, LANES), 1)
    match = jnp.bitwise_and(source, 2 * count - 1) == jnp.bitwise_and(target, GROUP_LANES - 1)
    fold = jnp.logical_and(source < used, match).astype(BF)
    found = dot(kept.astype(BF), fold).reshape(clusters, cap // GROUP, GROUP, LANES)
    group = iota((clusters, GROUP, LANES), 2) // GROUP_LANES
    meta = found[:, 0]
    for g in range(1, cap // GROUP):
        meta = jnp.where(group == g, found[:, g], meta)
    send_ref[:, width // LANES * cap :, :] = meta.astype(BF)
    got = dot(pick, embed_ref[...]).astype(BF)
    for k in range(width // LANES):
        part = got[:, k * LANES : (k + 1) * LANES]
        send_ref[:, k * cap : (k + 1) * cap, :] = part.reshape(clusters, cap, LANES)


def assemble(recv_ref, rows_ref):
    total, width = rows_ref.shape
    for k in range(width // LANES):
        part = recv_ref[:, k * CAP : (k + 1) * CAP, :]
        rows_ref[:, k * LANES : (k + 1) * LANES] = part.reshape(total, LANES)


def target_bits(count, recv_ref, bits_ref, width):
    sources = recv_ref.shape[0]
    step = 8
    tall = step * GROUP
    for start in range(0, sources, step):
        meta = recv_ref[start : start + step, width // LANES * CAP :, :]
        meta = meta.astype(F32).astype(jnp.int32).reshape(tall, LANES)
        lane = iota((tall, LANES), 1)
        groups = []
        for g in range(CAP // GROUP):
            base = g * GROUP_LANES
            bits = jnp.zeros((tall, LANES), jnp.int32)
            for p in range(count):
                value = meta[:, base + p : base + p + 1]
                place = meta[:, base + count + p : base + count + p + 1]
                bits = jnp.bitwise_or(bits, jnp.where(place == lane, value, 0))
            groups.append(bits.reshape(step, GROUP, LANES))
        both = jnp.concatenate(groups, axis=1)
        bits_ref[start * CAP : (start + step) * CAP] = both.reshape(step * CAP, LANES)


def score_kernel(
    count, recv_ref, table_ref, pads_ref, back_out, give_out, keep_out,
    weight_ref, back_ref, rows_ref, bits_ref, s_ref, error_ref, relu_ref, prod_ref, sum_ref,
    weight_sem, error_sem, back_sem, rows_sem,
):
    sources = recv_ref.shape[0]
    total, width = rows_ref.shape
    chunks = weight_ref.shape[0] // CHUNK
    loads = []
    for i in range(chunks):
        here = slice(i * CHUNK, (i + 1) * CHUNK)
        load = pltpu.make_async_copy(table_ref.at[here], weight_ref.at[here], weight_sem.at[i])
        load.start()
        loads.append(load)
    assemble(recv_ref, rows_ref)
    spare = pltpu.make_async_copy(rows_ref, give_out.at[:, keep_out.shape[1] :], rows_sem)
    spare.start()
    target_bits(count, recv_ref, bits_ref, width)
    copies = [spare]

    def score(i, at):
        chunk = weight_ref[i * CHUNK : (i + 1) * CHUNK]
        s_ref[i % 2, at] = dot(rows_ref[at], chunk, NT)

    def pointwise(i, at):
        for start in range(at.start, at.stop, TALL):
            here = slice(start, start + TALL)
            bits = bits_ref[here]
            if i == 0:
                relu = jnp.zeros((TALL, LANES), F32)
                prod = jnp.ones((TALL, LANES), F32)
                summed = relu
            else:
                relu, prod, summed = relu_ref[here], prod_ref[here], sum_ref[here]
            for part in range(CHUNK // LANES):
                column = i * CHUNK + part * LANES
                s = s_ref[i % 2, here, part * LANES : (part + 1) * LANES]
                hit = lax.shift_left(bits, 31 - column // LANES) < 0
                size = jnp.abs(s)
                e = jnp.exp2(size * -LOG2E)
                d = 1.0 + e
                r = pl.reciprocal(d, approx=True)
                up = jnp.logical_xor(s >= 0.0, hit)
                chance = jnp.where(up, r, e * r)
                error = jnp.where(hit, -chance, chance)
                error_ref[here, column : column + LANES] = error.astype(BF)
                relu = relu + jnp.where(up, size, 0.0)
                prod = prod * d
                summed = summed + e
            relu_ref[here] = relu
            prod_ref[here] = prod
            sum_ref[here] = summed

    def flush(at):
        half = keep_out.shape[1]
        for k, out in enumerate((give_out, keep_out)):
            copy = pltpu.make_async_copy(
                error_ref.at[at, k * half : (k + 1) * half],
                out.at[at, :half],
                error_sem.at[2 * (at.start // BLOCK) + k],
            )
            copy.start()
            copies.append(copy)

    blocks = [slice(k, k + BLOCK) for k in range(0, total, BLOCK)]
    for i in range(-1, chunks):
        if i + 1 < chunks:
            loads[i + 1].wait()
        for at in blocks:
            if i + 1 < chunks:
                score(i + 1, at)
            if i >= 0:
                pointwise(i, at)
    for at in blocks:
        flush(at)

    summed = sum_ref[...] - pads_ref[0:1]
    tail = jnp.where(summed < 4e-4, summed, jnp.log(prod_ref[...] * pads_ref[1:2]))
    loss = jnp.sum(relu_ref[...] + tail, axis=1, keepdims=True)
    first = loss.astype(BF).astype(F32)
    second = (loss - first).astype(BF).astype(F32)
    third = loss - first - second
    part = jnp.bitwise_and(iota((total, LANES), 1), 3)
    terms = jnp.where(part == 2, third, 0.0)
    terms = jnp.where(part == 1, second, terms)
    terms = jnp.where(part == 0, first, terms)
    terms = terms.reshape(sources, CAP // GROUP, GROUP, LANES)
    group = lax.shift_right_logical(iota((sources, GROUP, LANES), 2), 2)
    mixed = jnp.zeros((sources, GROUP, LANES), F32)
    for g in range(CAP // GROUP):
        mixed = jnp.where(group == g, terms[:, g], mixed)
    back_ref[:, width // LANES * CAP :, :] = mixed.astype(BF)
    for at in blocks:
        first, last = at.start // CAP, at.stop // CAP
        grads = dot(error_ref[at], weight_ref[...]).astype(BF)
        for k in range(width // LANES):
            part = grads[:, k * LANES : (k + 1) * LANES]
            back_ref[first:last, k * CAP : (k + 1) * CAP, :] = part.reshape(last - first, CAP, LANES)
        copy = pltpu.make_async_copy(
            back_ref.at[first:last], back_out.at[first:last], back_sem.at[at.start // BLOCK]
        )
        copy.start()
        copies.append(copy)
    for copy in copies:
        copy.wait()


def weight_kernel(blocks, mine_in, other_in, mine_rows, *rest):
    outs, scratch = rest[: len(blocks)], rest[len(blocks) :]
    mine_ref, other_ref, partner_ref, rows_ref, held_ref, load_sem, store_sem = scratch
    half = mine_in.shape[1]
    block, width = outs[0].shape
    first = min(blocks) * block // LANES * LANES
    last = -(-(max(blocks) + 1) * block // LANES) * LANES
    here = slice(first, last)
    loads = []
    for source, target in (
        (mine_in.at[:, here], mine_ref),
        (other_in.at[:, half:], partner_ref),
        (other_in.at[:, here], other_ref),
    ):
        load = pltpu.make_async_copy(source, target, load_sem.at[len(loads)])
        load.start()
        loads.append(load)
    assemble(mine_rows, rows_ref)
    stores = []
    for i, k in enumerate(blocks):
        at = slice(k * block - first, (k + 1) * block - first)
        if i == 0:
            loads[0].wait()
        grads = dot(mine_ref[:, at], rows_ref[...], TN)
        if i == 0:
            loads[1].wait()
            loads[2].wait()
        grads += dot(other_ref[:, at], partner_ref[...], TN)
        held_ref[i] = grads.astype(held_ref.dtype)
        store = pltpu.make_async_copy(held_ref.at[i], outs[i], store_sem.at[i])
        store.start()
        stores.append(store)
    for store in stores:
        store.wait()


def combine_kernel(
    scale, got_ref, pick_in, share_in, first_in, second_in, third_in,
    grad_out, loss_ref, weight_ref, pick_ref, share_ref, parts_ref, grad_ref, sem,
):
    clusters = got_ref.shape[0]
    rows, width = grad_ref.shape
    loads = [pltpu.make_async_copy(pick_in, pick_ref, sem.at[0])]
    loads.append(pltpu.make_async_copy(share_in, share_ref, sem.at[1]))
    for k, part in enumerate((first_in, second_in, third_in)):
        loads.append(pltpu.make_async_copy(part, parts_ref.at[k], sem.at[2 + k]))
    for load in loads:
        load.start()
    parts = []
    for k in range(width // LANES):
        part = got_ref[:, k * CAP : (k + 1) * CAP, :]
        parts.append(part.reshape(clusters * CAP, LANES))
    terms = got_ref[:, width // LANES * CAP :, :].astype(F32)
    group = lax.shift_right_logical(iota((clusters, GROUP, LANES), 2), 2)
    spread = [jnp.where(group == g, terms, 0.0) for g in range(CAP // GROUP)]
    parts.append(jnp.stack(spread, axis=1).reshape(clusters * CAP, LANES).astype(BF))
    loads[0].wait()
    summed = dot(pick_ref[...], jnp.concatenate(parts, axis=1), TN)
    grad_ref[...] = summed[:, :width].astype(BF)
    store = pltpu.make_async_copy(grad_ref, grad_out, sem.at[len(loads)])
    store.start()
    loss_ref[...] = jnp.sum(summed[:, width:].T, axis=0, keepdims=True) * scale
    for load in loads[1:]:
        load.wait()
    share = share_ref[...]
    for k in range(parts_ref.shape[0]):
        share += parts_ref[k].astype(F32)
    weight_ref[...] = share[: weight_ref.shape[0]].astype(BF)
    store.wait()


def whole(shape, dtype):
    return jax.ShapeDtypeStruct(shape, dtype)


VM = pl.BlockSpec(memory_space=pltpu.VMEM)
SM = pl.BlockSpec(memory_space=pltpu.SMEM)
HBM = pl.BlockSpec(memory_space=pltpu.HBM)


def in_hbm(array):
    return pltpu.with_memory_space_constraint(array, pltpu.HBM)


PARAMS = pltpu.CompilerParams(vmem_limit_bytes=VMEM_LIMIT)


def local(embed, weights, shortlist, positives):
    rows, width = embed.shape
    slots_k = shortlist.shape[1]
    count = positives.shape[1]
    _, labels, _ = weights.shape
    clusters = lax.axis_size("clus")
    shards = lax.axis_size("rows")
    shape = (clusters, width // LANES * CAP + GROUP, LANES)
    total = clusters * CAP
    block = labels // shards
    tall = padded(block)
    half = shards // 2

    place = lax.axis_index("rows")
    core, x = place % 2, place // 2
    order = [((x + k) % half) * 2 + side for side in (1 - core, core) for k in range(half)]

    send, pick = pl.pallas_call(
        functools.partial(pack_kernel, labels, shards),
        out_shape=(whole(shape, BF), whole((total, rows), BF)),
        in_specs=[VM] * 3,
        out_specs=(VM, VM),
        compiler_params=pltpu.CompilerParams(vmem_limit_bytes=60 * 1024 * 1024),
    )(embed, shortlist.T, positives.T)
    recv = lax.all_to_all(send, "clus", 0, 0, tiled=True)

    table = jnp.pad(weights.reshape(shards, block, width), ((0, 0), (0, tall - block), (0, 0)))
    table = jnp.stack([lax.dynamic_index_in_dim(table, k, 0, keepdims=False) for k in order])
    table = table.reshape(shards * tall, width)
    column = np.arange(shards * tall)
    pads = np.bincount(column[column % tall >= block] % LANES, minlength=LANES)
    pads = np.stack([pads, 0.5**pads]).astype(np.float32)
    back, give, keep = pl.pallas_call(
        functools.partial(score_kernel, count),
        out_shape=(
            pltpu.HBM(shape, BF),
            pltpu.HBM((total, half * tall + width), BF),
            pltpu.HBM((total, half * tall), BF),
        ),
        in_specs=[VM, HBM, VM],
        out_specs=(HBM, HBM, HBM),
        scratch_shapes=[
            pltpu.VMEM((shards * tall, width), BF),
            pltpu.VMEM(shape, BF),
            pltpu.VMEM((total, width), BF),
            pltpu.VMEM((total, LANES), jnp.int32),
            pltpu.VMEM((2, total, CHUNK), F32),
            pltpu.VMEM((total, shards * tall), BF),
            pltpu.VMEM((total, LANES), F32),
            pltpu.VMEM((total, LANES), F32),
            pltpu.VMEM((total, LANES), F32),
            pltpu.SemaphoreType.DMA((shards * tall // CHUNK,)),
            pltpu.SemaphoreType.DMA((2 * total // BLOCK,)),
            pltpu.SemaphoreType.DMA((total // BLOCK,)),
            pltpu.SemaphoreType.DMA,
        ],
        compiler_params=PARAMS,
    )(recv, in_hbm(table), jnp.asarray(pads))
    got = lax.all_to_all(back, "clus", 0, 0, tiled=True)

    swap = [(i, i ^ 1) for i in range(shards)]
    other = lax.ppermute(give, "rows", swap)
    def weight_part(blocks, dtype):
        first = min(blocks) * tall // LANES * LANES
        size = -(-(max(blocks) + 1) * tall // LANES) * LANES - first
        return pl.pallas_call(
            functools.partial(weight_kernel, blocks),
            out_shape=(pltpu.HBM((tall, width), dtype),) * len(blocks),
            in_specs=[HBM, HBM, VM],
            out_specs=(HBM,) * len(blocks),
            scratch_shapes=[
                pltpu.VMEM((total, size), BF),
                pltpu.VMEM((total, size), BF),
                pltpu.VMEM((total, width), BF),
                pltpu.VMEM((total, width), BF),
                pltpu.VMEM((len(blocks), tall, width), dtype),
                pltpu.SemaphoreType.DMA((3,)),
                pltpu.SemaphoreType.DMA((len(blocks),)),
            ],
            compiler_params=pltpu.CompilerParams(vmem_limit_bytes=20 * 1024 * 1024),
            cost_estimate=pl.CostEstimate(flops=1, bytes_accessed=1, transcendentals=0),
        )(in_hbm(keep), in_hbm(other), recv)

    away = tuple(range(1, half))
    arrived = []
    for k, piece in zip(away, weight_part(away, BF)):
        perm = [(i, (i + 2 * k) % shards) for i in range(shards)]
        arrived.append(lax.ppermute(piece, "rows", perm))
    (share,) = weight_part((0,), F32)
    row_grad, row_loss, weight_grad = pl.pallas_call(
        functools.partial(combine_kernel, 1.0 / (slots_k * labels)),
        out_shape=(
            pltpu.HBM((rows, width), BF),
            whole((1, rows), F32),
            whole((block, width), BF),
        ),
        in_specs=[VM] + [HBM] * 5,
        out_specs=(HBM, VM, VM),
        scratch_shapes=[
            pltpu.VMEM((total, rows), BF),
            pltpu.VMEM((tall, width), F32),
            pltpu.VMEM((half - 1, tall, width), BF),
            pltpu.VMEM((rows, width), BF),
            pltpu.SemaphoreType.DMA((6,)),
        ],
        compiler_params=pltpu.CompilerParams(vmem_limit_bytes=24 * 1024 * 1024),
    )(got, in_hbm(pick), in_hbm(share), *[in_hbm(part) for part in arrived])
    return row_grad, row_loss.reshape(rows), weight_grad[None]


def solution(mesh):
    placed = (
        P(("rows", "clus"), None),
        P("clus", None, None),
        P(("rows", "clus"), None),
        P(("rows", "clus"), None),
    )
    return jax.shard_map(
        local,
        mesh=mesh,
        in_specs=placed,
        out_specs=(P(("rows", "clus"), None), P(("rows", "clus")), P("clus", "rows", None)),
        check_vma=False,
    )
```

```python
import functools
import jax
import jax.numpy as jnp
import numpy as np
from jax import lax
from jax.experimental import pallas as pl
from jax.experimental.pallas import tpu as pltpu
from jax.sharding import PartitionSpec as P

BF = jnp.bfloat16
F32 = jnp.float32
LANES = 128
CHUNK = 512
CAP = 32
GROUP = 8
GROUP_LANES = 32
VMEM_LIMIT = 40 * 1024 * 1024
TALL = 16
BLOCK = 512
LOG2E = 1.4426950408889634

NT = (((1,), (1,)), ((), ()))
TN = (((0,), (0,)), ((), ()))
NN = (((1,), (0,)), ((), ()))


def dot(a, b, dims=NN):
    return lax.dot_general(a, b, dims, preferred_element_type=F32)


def iota(shape, dim):
    return lax.broadcasted_iota(jnp.int32, shape, dim)


def padded(block):
    return -(-block // 32) * 32


def pack_kernel(
    labels, shards, embed_ref, short_ref, pos_ref, send_ref, pick_ref
):
    rows, width = embed_ref.shape
    slots_k = short_ref.shape[0]
    clusters = send_ref.shape[0]
    cap = CAP
    block = labels // shards
    place = lax.axis_index("rows")
    core, x = lax.rem(place, 2), lax.div(place, 2)
    half = shards // 2
    shift = []
    for b in range(shards):
        step = lax.rem(b // 2 - x + half, half)
        slot = step + jnp.where(core == b % 2, half, 0)
        shift.append(padded(block) * slot - block * b)
    short = short_ref[...]
    pos = pos_ref[...]
    count = pos.shape[0]
    cluster_id = iota((clusters, rows), 0)
    member = jnp.zeros((clusters, rows), F32)
    for j in range(slots_k):
        member += (short[j : j + 1, :] == cluster_id).astype(F32)
    before = (iota((rows, rows), 0) < iota((rows, rows), 1)).astype(BF)
    rank = dot(member.astype(BF), before)
    code = jnp.where(member > 0.5, rank, -1.0)
    slot = iota((clusters, cap, rows), 1).astype(F32)
    pick = (code[:, None, :] == slot).astype(F32)
    pick = pick.reshape(clusters * cap, rows).astype(BF)
    pick_ref[...] = pick
    values, names = [], []
    for j in range(slots_k):
        local = pos - j * labels
        inside = jnp.logical_and(local >= 0, local < labels)
        column = local + shift[0]
        for b in range(1, shards):
            column += jnp.where(local >= b * block, shift[b] - shift[b - 1], 0)
        column = jnp.where(inside, column, 0)
        bit = lax.shift_left(jnp.ones_like(column), lax.shift_right_logical(column, 7))
        values.append(jnp.where(inside, bit, 0).astype(F32))
        values.append(jnp.bitwise_and(column, LANES - 1).astype(F32))
        names.append(jnp.broadcast_to(short[j : j + 1, :], (2 * count, rows)).astype(F32))
    used = 2 * count * slots_k
    rest = jnp.zeros((LANES - used, rows), F32)
    values = jnp.concatenate(values + [rest], axis=0).astype(BF)
    names = jnp.concatenate(names + [rest], axis=0).astype(BF)
    got_values = dot(pick, values, NT)
    got_names = dot(pick, names, NT)
    own = lax.shift_right_logical(iota(got_values.shape, 0), 5).astype(F32)
    kept = jnp.where(got_names == own, got_values, 0.0)
    source = iota((LANES, LANES), 0)
    target = iota((LANES, LANES), 1)
    match = jnp.bitwise_and(source, 2 * count - 1) == jnp.bitwise_and(target, GROUP_LANES - 1)
    fold = jnp.logical_and(source < used, match).astype(BF)
    found = dot(kept.astype(BF), fold).reshape(clusters, cap // GROUP, GROUP, LANES)
    group = iota((clusters, GROUP, LANES), 2) // GROUP_LANES
    meta = found[:, 0]
    for g in range(1, cap // GROUP):
        meta = jnp.where(group == g, found[:, g], meta)
    send_ref[:, width // LANES * cap :, :] = meta.astype(BF)
    got = dot(pick, embed_ref[...]).astype(BF)
    for k in range(width // LANES):
        part = got[:, k * LANES : (k + 1) * LANES]
        send_ref[:, k * cap : (k + 1) * cap, :] = part.reshape(clusters, cap, LANES)


def assemble(recv_ref, rows_ref):
    total, width = rows_ref.shape
    for k in range(width // LANES):
        part = recv_ref[:, k * CAP : (k + 1) * CAP, :]
        rows_ref[:, k * LANES : (k + 1) * LANES] = part.reshape(total, LANES)


def target_bits(count, recv_ref, bits_ref, width):
    sources = recv_ref.shape[0]
    step = 8
    tall = step * GROUP
    for start in range(0, sources, step):
        meta = recv_ref[start : start + step, width // LANES * CAP :, :]
        meta = meta.astype(F32).astype(jnp.int32).reshape(tall, LANES)
        lane = iota((tall, LANES), 1)
        groups = []
        for g in range(CAP // GROUP):
            base = g * GROUP_LANES
            bits = jnp.zeros((tall, LANES), jnp.int32)
            for p in range(count):
                value = meta[:, base + p : base + p + 1]
                place = meta[:, base + count + p : base + count + p + 1]
                bits = jnp.bitwise_or(bits, jnp.where(place == lane, value, 0))
            groups.append(bits.reshape(step, GROUP, LANES))
        both = jnp.concatenate(groups, axis=1)
        bits_ref[start * CAP : (start + step) * CAP] = both.reshape(step * CAP, LANES)


def score_kernel(
    count, recv_ref, table_ref, pads_ref, back_out, give_out, keep_out,
    weight_ref, back_ref, rows_ref, bits_ref, s_ref, error_ref, relu_ref, prod_ref, sum_ref,
    weight_sem, error_sem, back_sem, rows_sem,
):
    sources = recv_ref.shape[0]
    total, width = rows_ref.shape
    labels = weight_ref.shape[0]
    bounds = [slice(k, min(k + CHUNK, labels)) for k in range(0, labels, CHUNK)]
    chunks = len(bounds)
    loads = []
    for i, here in enumerate(bounds):
        load = pltpu.make_async_copy(table_ref.at[here], weight_ref.at[here], weight_sem.at[i])
        load.start()
        loads.append(load)
    assemble(recv_ref, rows_ref)
    spare = pltpu.make_async_copy(rows_ref, give_out.at[:, keep_out.shape[1] :], rows_sem)
    spare.start()
    target_bits(count, recv_ref, bits_ref, width)
    copies = [spare]

    def score(i, at):
        size = bounds[i].stop - bounds[i].start
        s_ref[i % 2, at, :size] = dot(rows_ref[at], weight_ref[bounds[i]], NT)

    def pointwise(i, at):
        for start in range(at.start, at.stop, TALL):
            here = slice(start, start + TALL)
            bits = bits_ref[here]
            if i == 0:
                relu = jnp.zeros((TALL, LANES), F32)
                prod = jnp.ones((TALL, LANES), F32)
                summed = relu
            else:
                relu, prod, summed = relu_ref[here], prod_ref[here], sum_ref[here]
            for column in range(bounds[i].start, bounds[i].stop, LANES):
                offset = column - bounds[i].start
                s = s_ref[i % 2, here, offset : offset + LANES]
                hit = lax.shift_left(bits, 31 - column // LANES) < 0
                size = jnp.abs(s)
                e = jnp.exp2(size * -LOG2E)
                d = 1.0 + e
                r = pl.reciprocal(d, approx=True)
                up = jnp.logical_xor(s >= 0.0, hit)
                chance = jnp.where(up, r, e * r)
                error = jnp.where(hit, -chance, chance)
                error_ref[here, column : column + LANES] = error.astype(BF)
                relu = relu + jnp.where(up, size, 0.0)
                prod = prod * d
                summed = summed + e
            relu_ref[here] = relu
            prod_ref[here] = prod
            sum_ref[here] = summed

    def flush(at):
        half = keep_out.shape[1]
        for k, out in enumerate((give_out, keep_out)):
            copy = pltpu.make_async_copy(
                error_ref.at[at, k * half : (k + 1) * half],
                out.at[at, :half],
                error_sem.at[2 * (at.start // BLOCK) + k],
            )
            copy.start()
            copies.append(copy)

    blocks = [slice(k, k + BLOCK) for k in range(0, total, BLOCK)]
    for i in range(-1, chunks):
        if i + 1 < chunks:
            loads[i + 1].wait()
        for at in blocks:
            if i + 1 < chunks:
                score(i + 1, at)
            if i >= 0:
                pointwise(i, at)
    for at in blocks:
        flush(at)

    summed = sum_ref[...] - pads_ref[0:1]
    tail = jnp.where(summed < 4e-4, summed, jnp.log(prod_ref[...] * pads_ref[1:2]))
    loss = jnp.sum(relu_ref[...] + tail, axis=1, keepdims=True)
    first = loss.astype(BF).astype(F32)
    second = (loss - first).astype(BF).astype(F32)
    third = loss - first - second
    part = jnp.bitwise_and(iota((total, LANES), 1), 3)
    terms = jnp.where(part == 2, third, 0.0)
    terms = jnp.where(part == 1, second, terms)
    terms = jnp.where(part == 0, first, terms)
    terms = terms.reshape(sources, CAP // GROUP, GROUP, LANES)
    group = lax.shift_right_logical(iota((sources, GROUP, LANES), 2), 2)
    mixed = jnp.zeros((sources, GROUP, LANES), F32)
    for g in range(CAP // GROUP):
        mixed = jnp.where(group == g, terms[:, g], mixed)
    back_ref[:, width // LANES * CAP :, :] = mixed.astype(BF)
    for at in blocks:
        first, last = at.start // CAP, at.stop // CAP
        grads = dot(error_ref[at], weight_ref[...]).astype(BF)
        for k in range(width // LANES):
            part = grads[:, k * LANES : (k + 1) * LANES]
            back_ref[first:last, k * CAP : (k + 1) * CAP, :] = part.reshape(last - first, CAP, LANES)
        copy = pltpu.make_async_copy(
            back_ref.at[first:last], back_out.at[first:last], back_sem.at[at.start // BLOCK]
        )
        copy.start()
        copies.append(copy)
    for copy in copies:
        copy.wait()


def weight_kernel(blocks, mine_in, other_in, mine_rows, *rest):
    outs, scratch = rest[: len(blocks)], rest[len(blocks) :]
    mine_ref, other_ref, partner_ref, rows_ref, held_ref, load_sem, store_sem = scratch
    half = mine_in.shape[1]
    block, width = outs[0].shape
    first = min(blocks) * block // LANES * LANES
    last = -(-(max(blocks) + 1) * block // LANES) * LANES
    here = slice(first, last)
    loads = []
    for source, target in (
        (mine_in.at[:, here], mine_ref),
        (other_in.at[:, half:], partner_ref),
        (other_in.at[:, here], other_ref),
    ):
        load = pltpu.make_async_copy(source, target, load_sem.at[len(loads)])
        load.start()
        loads.append(load)
    assemble(mine_rows, rows_ref)
    stores = []
    for i, k in enumerate(blocks):
        at = slice(k * block - first, (k + 1) * block - first)
        if i == 0:
            loads[0].wait()
        grads = dot(mine_ref[:, at], rows_ref[...], TN)
        if i == 0:
            loads[1].wait()
            loads[2].wait()
        grads += dot(other_ref[:, at], partner_ref[...], TN)
        held_ref[i] = grads.astype(held_ref.dtype)
        store = pltpu.make_async_copy(held_ref.at[i], outs[i], store_sem.at[i])
        store.start()
        stores.append(store)
    for store in stores:
        store.wait()


def combine_kernel(
    scale, got_ref, pick_in, share_in, first_in, second_in, third_in,
    grad_out, loss_ref, weight_ref, pick_ref, share_ref, parts_ref, grad_ref, sem,
):
    clusters = got_ref.shape[0]
    rows, width = grad_ref.shape
    loads = [pltpu.make_async_copy(pick_in, pick_ref, sem.at[0])]
    loads.append(pltpu.make_async_copy(share_in, share_ref, sem.at[1]))
    for k, part in enumerate((first_in, second_in, third_in)):
        loads.append(pltpu.make_async_copy(part, parts_ref.at[k], sem.at[2 + k]))
    for load in loads:
        load.start()
    parts = []
    for k in range(width // LANES):
        part = got_ref[:, k * CAP : (k + 1) * CAP, :]
        parts.append(part.reshape(clusters * CAP, LANES))
    terms = got_ref[:, width // LANES * CAP :, :].astype(F32)
    group = lax.shift_right_logical(iota((clusters, GROUP, LANES), 2), 2)
    spread = [jnp.where(group == g, terms, 0.0) for g in range(CAP // GROUP)]
    parts.append(jnp.stack(spread, axis=1).reshape(clusters * CAP, LANES).astype(BF))
    loads[0].wait()
    summed = dot(pick_ref[...], jnp.concatenate(parts, axis=1), TN)
    grad_ref[...] = summed[:, :width].astype(BF)
    store = pltpu.make_async_copy(grad_ref, grad_out, sem.at[len(loads)])
    store.start()
    loss_ref[...] = jnp.sum(summed[:, width:].T, axis=0, keepdims=True) * scale
    for load in loads[1:]:
        load.wait()
    share = share_ref[...]
    for k in range(parts_ref.shape[0]):
        share += parts_ref[k].astype(F32)
    weight_ref[...] = share[: weight_ref.shape[0]].astype(BF)
    store.wait()


def whole(shape, dtype):
    return jax.ShapeDtypeStruct(shape, dtype)


VM = pl.BlockSpec(memory_space=pltpu.VMEM)
SM = pl.BlockSpec(memory_space=pltpu.SMEM)
HBM = pl.BlockSpec(memory_space=pltpu.HBM)


def in_hbm(array):
    return pltpu.with_memory_space_constraint(array, pltpu.HBM)


PARAMS = pltpu.CompilerParams(vmem_limit_bytes=VMEM_LIMIT)


def local(embed, weights, shortlist, positives):
    rows, width = embed.shape
    slots_k = shortlist.shape[1]
    count = positives.shape[1]
    _, labels, _ = weights.shape
    clusters = lax.axis_size("clus")
    shards = lax.axis_size("rows")
    shape = (clusters, width // LANES * CAP + GROUP, LANES)
    total = clusters * CAP
    block = labels // shards
    tall = padded(block)
    half = shards // 2

    place = lax.axis_index("rows")
    core, x = place % 2, place // 2
    order = [((x + k) % half) * 2 + side for side in (1 - core, core) for k in range(half)]

    send, pick = pl.pallas_call(
        functools.partial(pack_kernel, labels, shards),
        out_shape=(whole(shape, BF), whole((total, rows), BF)),
        in_specs=[VM] * 3,
        out_specs=(VM, VM),
        compiler_params=pltpu.CompilerParams(vmem_limit_bytes=60 * 1024 * 1024),
    )(embed, shortlist.T, positives.T)
    recv = lax.all_to_all(send, "clus", 0, 0, tiled=True)

    table = jnp.pad(weights.reshape(shards, block, width), ((0, 0), (0, tall - block), (0, 0)))
    table = jnp.stack([lax.dynamic_index_in_dim(table, k, 0, keepdims=False) for k in order])
    table = table.reshape(shards * tall, width)
    column = np.arange(shards * tall)
    pads = np.bincount(column[column % tall >= block] % LANES, minlength=LANES)
    pads = np.stack([pads, 0.5**pads]).astype(np.float32)
    back, give, keep = pl.pallas_call(
        functools.partial(score_kernel, count),
        out_shape=(
            pltpu.HBM(shape, BF),
            pltpu.HBM((total, half * tall + width), BF),
            pltpu.HBM((total, half * tall), BF),
        ),
        in_specs=[VM, HBM, VM],
        out_specs=(HBM, HBM, HBM),
        scratch_shapes=[
            pltpu.VMEM((shards * tall, width), BF),
            pltpu.VMEM(shape, BF),
            pltpu.VMEM((total, width), BF),
            pltpu.VMEM((total, LANES), jnp.int32),
            pltpu.VMEM((2, total, CHUNK), F32),
            pltpu.VMEM((total, shards * tall), BF),
            pltpu.VMEM((total, LANES), F32),
            pltpu.VMEM((total, LANES), F32),
            pltpu.VMEM((total, LANES), F32),
            pltpu.SemaphoreType.DMA((-(-shards * tall // CHUNK),)),
            pltpu.SemaphoreType.DMA((2 * total // BLOCK,)),
            pltpu.SemaphoreType.DMA((total // BLOCK,)),
            pltpu.SemaphoreType.DMA,
        ],
        compiler_params=PARAMS,
    )(recv, in_hbm(table), jnp.asarray(pads))
    got = lax.all_to_all(back, "clus", 0, 0, tiled=True)

    swap = [(i, i ^ 1) for i in range(shards)]
    other = lax.ppermute(give, "rows", swap)
    def weight_part(blocks, dtype):
        first = min(blocks) * tall // LANES * LANES
        size = -(-(max(blocks) + 1) * tall // LANES) * LANES - first
        return pl.pallas_call(
            functools.partial(weight_kernel, blocks),
            out_shape=(pltpu.HBM((tall, width), dtype),) * len(blocks),
            in_specs=[HBM, HBM, VM],
            out_specs=(HBM,) * len(blocks),
            scratch_shapes=[
                pltpu.VMEM((total, size), BF),
                pltpu.VMEM((total, size), BF),
                pltpu.VMEM((total, width), BF),
                pltpu.VMEM((total, width), BF),
                pltpu.VMEM((len(blocks), tall, width), dtype),
                pltpu.SemaphoreType.DMA((3,)),
                pltpu.SemaphoreType.DMA((len(blocks),)),
            ],
            compiler_params=pltpu.CompilerParams(vmem_limit_bytes=20 * 1024 * 1024),
            cost_estimate=pl.CostEstimate(flops=1, bytes_accessed=1, transcendentals=0),
        )(in_hbm(keep), in_hbm(other), recv)

    away = tuple(range(1, half))
    arrived = []
    for k, piece in zip(away, weight_part(away, BF)):
        perm = [(i, (i + 2 * k) % shards) for i in range(shards)]
        arrived.append(lax.ppermute(piece, "rows", perm))
    (share,) = weight_part((0,), F32)
    row_grad, row_loss, weight_grad = pl.pallas_call(
        functools.partial(combine_kernel, 1.0 / (slots_k * labels)),
        out_shape=(
            pltpu.HBM((rows, width), BF),
            whole((1, rows), F32),
            whole((block, width), BF),
        ),
        in_specs=[VM] + [HBM] * 5,
        out_specs=(HBM, VM, VM),
        scratch_shapes=[
            pltpu.VMEM((total, rows), BF),
            pltpu.VMEM((tall, width), F32),
            pltpu.VMEM((half - 1, tall, width), BF),
            pltpu.VMEM((rows, width), BF),
            pltpu.SemaphoreType.DMA((6,)),
        ],
        compiler_params=pltpu.CompilerParams(vmem_limit_bytes=24 * 1024 * 1024),
    )(got, in_hbm(pick), in_hbm(share), *[in_hbm(part) for part in arrived])
    return row_grad, row_loss.reshape(rows), weight_grad[None]


def solution(mesh):
    placed = (
        P(("rows", "clus"), None),
        P("clus", None, None),
        P(("rows", "clus"), None),
        P(("rows", "clus"), None),
    )
    return jax.shard_map(
        local,
        mesh=mesh,
        in_specs=placed,
        out_specs=(P(("rows", "clus"), None), P(("rows", "clus")), P("clus", "rows", None)),
        check_vma=False,
    )
```
